32 devices in a mesh: dp: 8 (over z, x), tensor: 4 (over y, core).
Axes of the slice: x: 2, y: 2, z: 4, core: 2. Of those that a mesh axis runs over, the one named last changes fastest.
Arguments:
- tokens: bfloat16 [8192, 768], P('dp'), may hold values from -6 to 6
- first_gain: float32 [768], replicated, may hold values from 0.1 to 1.9
- joint_weight: bfloat16 [768, 3, 768], P(None, None, 'tensor'), may hold values from -0.21875 to 0.21875
- output_weight: bfloat16 [768, 768], P('tensor'), may hold values from -4 to 4
- second_gain: float32 [768], replicated, may hold values from 0.1 to 1.9
- expand_weight: bfloat16 [768, 2, 1152], P(None, None, 'tensor'), may hold values from -0.21875 to 0.21875
- shrink_weight: bfloat16 [1152, 768], P('tensor'), may hold values from -0.1875 to 0.1875
- cotangent: bfloat16 [8192, 768], P(('dp', 'tensor')), may hold values from -6 to 6
Outputs:
- block_out: bfloat16 [8192, 768], P(('dp', 'tensor'))
- grad_tokens: float32 [8192, 768], P(('dp', 'tensor'))
- grad_first_gain: float32 [768], replicated
- grad_joint_weight: float32 [768, 3, 768], P(None, None, 'tensor')
- grad_output_weight: float32 [768, 768], P('tensor')
- grad_second_gain: float32 [768], replicated
- grad_expand_weight: float32 [768, 2, 1152], P(None, None, 'tensor')
- grad_shrink_weight: float32 [1152, 768], P('tensor')
The draws below stay inside these ranges and needn't reach their ends.
All inputs are finite; a program needn't handle non-finite values.
Results may differ from the reference program's by a relative error of at most 0.025.
Values may be sent and summed in bfloat16 or wider, within the bound.
A program may use at most 128 MiB of HBM per device.

```python
import jax
import jax.numpy as jnp
from jax import lax

D = 768
HEADS = 12
HEAD_DIM = 64
FF = 1152
SEQ_LEN = 1024
SEQS = 8
TOKENS = 8192


def block_levels(stream_key, extent, shards, least, largest):
    loudness, own = 1.0, jax.random.fold_in(stream_key, 6)
    for dim, shards_of in shards:
        draws = jnp.exp(jax.random.uniform(jax.random.fold_in(own, dim), (shards_of,), jnp.float32, least / len(shards), largest / len(shards)))
        loudness = loudness * jnp.repeat(draws, extent[dim] // shards_of).reshape([-1 if axis == dim else 1 for axis in range(len(extent))])
    return loudness


def bell_draw(key, extent, scale, reach, cuts=(), held_as=jnp.bfloat16):
    array = jax.random.normal(key, extent, jnp.float32) * scale
    if len(cuts) > 0:
        array = block_levels(key, extent, cuts, -0.22, 0.18) * array
    return jnp.clip(array, min=-reach, max=reach).astype(held_as)


def setup_inputs(seed: int = 0) -> dict:
    seeds = jax.random.split(jax.random.key(seed), 9)
    tokens = bell_draw(seeds[0], (TOKENS, D), 1.0, 6.0, ((0, 8),))
    first_gain = jnp.clip(1.0 + 0.18 * jax.random.normal(seeds[1], (D,), jnp.float32), 0.1, 1.9)
    joint_weight = bell_draw(seeds[2], (D, 3, D), D ** -0.5, 0.21875, ((2, 4),))
    output_weight = bell_draw(seeds[3], (D, D), 2 ** -0.5, 4.0, ((0, 4),))
    second_gain = jnp.clip(1.0 + 0.18 * jax.random.normal(seeds[4], (D,), jnp.float32), 0.1, 1.9)
    expand_weight = bell_draw(seeds[5], (D, 2, FF), D ** -0.5, 0.21875, ((2, 4),))
    shrink_weight = bell_draw(seeds[6], (FF, D), FF ** -0.5, 0.1875, ((0, 4),))
    cotangent = bell_draw(seeds[7], (TOKENS, D), 1.0, 6.0, ((0, 32),))
    return {"tokens": tokens, "first_gain": first_gain, "joint_weight": joint_weight, "output_weight": output_weight, "second_gain": second_gain, "expand_weight": expand_weight, "shrink_weight": shrink_weight, "cotangent": cotangent}


@jax.custom_vjp
def low(v):
    return lax.optimization_barrier(v.astype(jnp.bfloat16)).astype(jnp.float32)

@jax.custom_vjp
def low_back(v):
    return v

def low_keep(v):
    return (low(v), None)

def low_pass(kept, grad):
    return (grad,)

def back_keep(v):
    return (v, None)

def back_low(kept, grad):
    return (low(grad),)
low.defvjp(low_keep, low_pass)
low_back.defvjp(back_keep, back_low)
HIGHEST_PRECISION = lax.Precision.HIGHEST
eps_norm = 1e-05
theta_base = 160000.0

def layer_norm(values, gain_vector):
    centred = values - lax.optimization_barrier(jnp.mean(values, axis=-1, keepdims=True))
    spread = lax.optimization_barrier(jnp.mean(centred * centred, axis=-1, keepdims=True))
    return centred * lax.rsqrt(spread + eps_norm) * gain_vector

def rotary_tables(seq_length, head_width):
    half_width = head_width // 2
    frequency = theta_base ** (-(jnp.arange(half_width, dtype=jnp.float32) * 2.0 / head_width))
    angles = jnp.arange(seq_length, dtype=jnp.float32)[:, None] * frequency[None, :]
    angles = jnp.concatenate([angles, angles], axis=1)
    return (jnp.cos(angles), jnp.sin(angles))

def rotate(values, cosine, sine_table):
    half_width = values.shape[-1] // 2
    turned = jnp.concatenate([-values[..., half_width:], values[..., :half_width]], axis=-1)
    return values * cosine[:, None, :] + turned * sine_table[:, None, :]

def sequence_layer(params, seq_rows):
    first_gain, joint_weight, output_weight, second_gain, expand_weight, shrink_weight = params
    seq_length = seq_rows.shape[0]
    score_scale = HEAD_DIM ** (-0.5)
    normed = low(layer_norm(seq_rows, first_gain))
    joint_out = jnp.dot(normed, joint_weight.reshape(D, 3 * D), precision=HIGHEST_PRECISION)
    joint_out = joint_out.reshape(seq_length, 3, HEADS, HEAD_DIM)
    cosine, sine_table = rotary_tables(seq_length, HEAD_DIM)
    query_rot = low(rotate(low_back(joint_out[:, 0]), cosine, sine_table))
    key_rot = low(rotate(low_back(joint_out[:, 1]), cosine, sine_table))
    values = low(low_back(joint_out[:, 2]))
    scores = low_back(jnp.einsum('qhd,khd->hqk', query_rot, key_rot, precision=HIGHEST_PRECISION) * score_scale)
    prob_table = low(jax.nn.softmax(scores, axis=-1))
    mixed_heads = jnp.einsum('hqk,khd->qhd', prob_table, values, precision=HIGHEST_PRECISION)
    mixed_heads = low(low_back(mixed_heads.reshape(seq_length, D)))
    branch = low_back(jnp.dot(mixed_heads, output_weight, precision=HIGHEST_PRECISION))
    middle = seq_rows + branch
    second = low(layer_norm(middle, second_gain))
    gate_up = jnp.dot(second, expand_weight.reshape(D, 2 * FF), precision=HIGHEST_PRECISION)
    gate_up = gate_up.reshape(seq_length, 2, FF)
    gate_part = low_back(gate_up[:, 0])
    up_part = low_back(gate_up[:, 1])
    hidden = low(jax.nn.gelu(gate_part, approximate=True) * up_part)
    return middle + jnp.dot(hidden, shrink_weight, precision=HIGHEST_PRECISION)

def reference(tokens, first_gain, joint_weight, output_weight, second_gain, expand_weight, shrink_weight, cotangent):
    params = (first_gain.astype(jnp.float32), joint_weight.astype(jnp.float32), output_weight.astype(jnp.float32), second_gain.astype(jnp.float32), expand_weight.astype(jnp.float32), shrink_weight.astype(jnp.float32))
    seq_rows = tokens.astype(jnp.float32).reshape(SEQS, SEQ_LEN, D)

    def forward(weights, all_rows):

        def single_seq(one_rows):
            return sequence_layer(weights, one_rows)
        return lax.map(jax.checkpoint(single_seq), all_rows)
    result, pullback = jax.vjp(forward, params, seq_rows)
    weight_grads, grad_rows = pullback(cotangent.astype(jnp.float32).reshape(SEQS, SEQ_LEN, D))
    return (result.reshape(TOKENS, D).astype(jnp.bfloat16), grad_rows.reshape(TOKENS, D), weight_grads[0], weight_grads[1], weight_grads[2], weight_grads[3], weight_grads[4], weight_grads[5])
```

```python
import functools

import jax
import jax.numpy as jnp
import numpy as np
from jax import lax
from jax.experimental import pallas as pl
from jax.experimental.pallas import tpu as pltpu
from jax.sharding import PartitionSpec as P

HEAD_DIM = 64
SEQ_LEN = 1024
EPS = 1e-05
THETA = 160000.0
SCALE = HEAD_DIM**-0.5
CHUNKS = 2
VMEM_LIMIT = 48 * 1024 * 1024
F32 = jnp.float32
BF16 = jnp.bfloat16
VMEM = pl.BlockSpec(memory_space=pltpu.VMEM)


def dot(a, b, dims=((1,), (0,))):
    return lax.dot_general(a, b, (dims, ((), ())), preferred_element_type=F32)


def norm_parts(values):
    centred = values - jnp.mean(values, axis=-1, keepdims=True)
    inverse = lax.rsqrt(jnp.mean(centred * centred, axis=-1, keepdims=True) + EPS)
    return centred * inverse, inverse


def norm_back(hat, inverse, gain, grad):
    scaled = grad * gain
    return inverse * (
        scaled
        - jnp.mean(scaled, axis=-1, keepdims=True)
        - hat * jnp.mean(scaled * hat, axis=-1, keepdims=True)
    )


def head_rows(array, head):
    index = lax.broadcasted_iota(jnp.int32, array.shape, 0) // HEAD_DIM
    return jnp.where(index == head, array, jnp.zeros_like(array))


def head_columns(array, head):
    index = lax.broadcasted_iota(jnp.int32, array.shape, 1) // HEAD_DIM
    return jnp.where(index == head, array, jnp.zeros_like(array))


def attend_kernel(heads, key, query_t, value_t, mixed_t, logsum):
    for head in range(heads):
        rows = slice(head * HEAD_DIM, (head + 1) * HEAD_DIM)
        scores = dot(key[...], head_rows(query_t[...], head)) * SCALE
        peak = jnp.max(scores, axis=0, keepdims=True)
        exps = jnp.exp(scores - peak)
        total = jnp.sum(exps, axis=0, keepdims=True)
        probs = (exps * (1.0 / total)).astype(BF16)
        mixed_t[rows, :] = dot(value_t[rows, :], probs).astype(BF16)
        logsum[head : head + 1, :] = peak + jnp.log(total)


def attend(key, query_t, value_t, heads, block):
    width, rows = query_t.shape
    per_seq = SEQ_LEN // block
    return pl.pallas_call(
        functools.partial(attend_kernel, heads),
        grid=(rows // block,),
        in_specs=[
            pl.BlockSpec((SEQ_LEN, width), lambda i: (i // per_seq, 0)),
            pl.BlockSpec((width, block), lambda i: (0, i)),
            pl.BlockSpec((width, SEQ_LEN), lambda i: (0, i // per_seq)),
        ],
        out_specs=[
            pl.BlockSpec((width, block), lambda i: (0, i)),
            pl.BlockSpec((8, block), lambda i: (0, i)),
        ],
        out_shape=[
            jax.ShapeDtypeStruct((width, rows), BF16),
            jax.ShapeDtypeStruct((8, rows), F32),
        ],
        compiler_params=pltpu.CompilerParams(vmem_limit_bytes=VMEM_LIMIT),
        name="attend",
    )(key, query_t, value_t)


def attend_back_kernel(
    heads, per_seq, key, key_t, query, query_t, value, grad, grad_t, logsum, dq_t, dk, dv
):
    @pl.when(pl.program_id(0) % per_seq == 0)
    def _():
        dk[...] = jnp.zeros_like(dk)
        dv[...] = jnp.zeros_like(dv)

    for head in range(heads):
        rows = slice(head * HEAD_DIM, (head + 1) * HEAD_DIM)
        scores = dot(key[...], head_rows(query_t[...], head)) * SCALE
        probs = jnp.exp(scores - logsum[head : head + 1, :])
        dprobs = dot(value[...], head_rows(grad_t[...], head))
        product = probs * dprobs
        delta = jnp.sum(product, axis=0, keepdims=True)
        dscores = (product - probs * delta).astype(BF16)
        dq_t[rows, :] = dot(key_t[rows, :], dscores) * SCALE
        dk[...] += dot(dscores, head_columns(query[...], head)) * SCALE
        dv[...] += dot(probs.astype(BF16), head_columns(grad[...], head))


def attend_back(key, key_t, query, query_t, value, grad, grad_t, logsum, heads, block):
    width, rows = query_t.shape
    per_seq = SEQ_LEN // block
    seq_down = pl.BlockSpec((SEQ_LEN, width), lambda i: (i // per_seq, 0))
    seq_across = pl.BlockSpec((width, SEQ_LEN), lambda i: (0, i // per_seq))
    down = pl.BlockSpec((block, width), lambda i: (i, 0))
    across = pl.BlockSpec((width, block), lambda i: (0, i))
    return pl.pallas_call(
        functools.partial(attend_back_kernel, heads, per_seq),
        grid=(rows // block,),
        in_specs=[
            seq_down,
            seq_across,
            down,
            across,
            seq_down,
            down,
            across,
            pl.BlockSpec((8, block), lambda i: (0, i)),
        ],
        out_specs=[across, seq_down, seq_down],
        out_shape=[
            jax.ShapeDtypeStruct((width, rows), F32),
            jax.ShapeDtypeStruct((rows, width), F32),
            jax.ShapeDtypeStruct((rows, width), F32),
        ],
        compiler_params=pltpu.CompilerParams(vmem_limit_bytes=VMEM_LIMIT),
        cost_estimate=pl.CostEstimate(
            flops=16 * rows * SEQ_LEN * width, bytes_accessed=16 * rows * width, transcendentals=0
        ),
        name="attend_back",
    )(key, key_t, query, query_t, value, grad, grad_t, logsum)


def exchange_kernel(sums, extras, gather, step, own, *refs):
    parts = refs[:sums]
    extra = refs[sums : sums + extras]
    outs = refs[sums + extras : -7]
    from_core, to_side, from_side, core_send, core_recv, side_send, side_recv = refs[-7:]
    me = lax.axis_index("tensor")
    side, core = me // 2, me % 2
    core_peer = side * 2 + (1 - core)
    side_peer = (1 - side) * 2 + core
    cross = (1 - side) * 2 + (1 - core)
    rows = own // CHUNKS

    barrier = pltpu.get_barrier_semaphore()
    for peer in (core_peer, side_peer):
        pl.semaphore_signal(
            barrier, inc=1, device_id={"tensor": peer}, device_id_type=pl.DeviceIdType.MESH
        )
    pl.semaphore_wait(barrier, 2)

    def at(owner, chunk):
        return pl.ds(pl.multiple_of(owner * own + chunk * rows, 16), rows)

    def here(chunk):
        return pl.ds(chunk * rows, rows)

    def send(src, dst, peer, slot, chunk, cores):
        copy = pltpu.make_async_remote_copy(
            src_ref=src,
            dst_ref=dst,
            send_sem=(core_send if cores else side_send).at[slot, chunk],
            recv_sem=(core_recv if cores else side_recv).at[slot, chunk],
            device_id={"tensor": peer},
            device_id_type=pl.DeviceIdType.MESH,
        )
        copy.start()
        return copy

    onward, mine, sideways = {}, {}, {}
    for slot in range(sums):
        for chunk in range(CHUNKS):
            onward[slot, chunk] = send(
                parts[slot].at[at(cross, chunk)],
                from_core.at[2 * slot, here(chunk)],
                core_peer,
                2 * slot,
                chunk,
                True,
            )
    for slot in range(sums):
        for chunk in range(CHUNKS):
            mine[slot, chunk] = send(
                parts[slot].at[at(core_peer, chunk)],
                from_core.at[2 * slot + 1, here(chunk)],
                core_peer,
                2 * slot + 1,
                chunk,
                True,
            )
    for slot in range(sums):
        for chunk in range(CHUNKS):
            onward[slot, chunk].wait_recv()
            to_side[slot, here(chunk)] = (
                parts[slot][at(side_peer, chunk)].astype(F32)
                + from_core[2 * slot, here(chunk)].astype(F32)
            ).astype(BF16)
            sideways[slot, chunk] = send(
                to_side.at[slot, here(chunk)],
                from_side.at[slot, here(chunk)],
                side_peer,
                slot,
                chunk,
                False,
            )
    sent = []
    gathered = []
    for chunk in range(CHUNKS):
        totals = []
        for slot in range(sums):
            mine[slot, chunk].wait_recv()
            sideways[slot, chunk].wait_recv()
            totals.append(
                parts[slot][at(me, chunk)].astype(F32)
                + from_core[2 * slot + 1, here(chunk)].astype(F32)
                + from_side[slot, here(chunk)].astype(F32)
            )
        result = step(chunk, at(me, chunk), here(chunk), totals, extra, outs)
        if gather:
            whole = outs[0]
            whole[at(me, chunk), :] = result
            block = whole.at[at(me, chunk)]
            over = send(block, block, side_peer, sums, chunk, False)
            near = send(block, block, core_peer, 2 * sums, chunk, True)
            gathered.append((over, near))
            sent += [over, near]
    relayed = []
    for chunk, (over, _) in enumerate(gathered):
        over.wait_recv()
        block = outs[0].at[at(side_peer, chunk)]
        relay = send(block, block, core_peer, 2 * sums + 1, chunk, True)
        relayed.append(relay)
        sent.append(relay)
    for _, near in gathered:
        near.wait_recv()
    for relay in relayed:
        relay.wait_recv()
    for copy in [*onward.values(), *mine.values(), *sideways.values(), *sent]:
        copy.wait_send()


def exchange(name, number, parts, extra, step, gather, out_shape):
    own = parts[0].shape[0] // 4
    width = parts[0].shape[1]
    sums = len(parts)
    core_slots = 2 * sums + (2 if gather else 0)
    side_slots = sums + (1 if gather else 0)
    return pl.pallas_call(
        functools.partial(exchange_kernel, sums, len(extra), gather, step, own),
        in_specs=[VMEM] * (sums + len(extra)),
        out_specs=[VMEM] * len(out_shape),
        out_shape=out_shape,
        scratch_shapes=[
            pltpu.VMEM((2 * sums, own, width), BF16),
            pltpu.VMEM((sums, own, width), BF16),
            pltpu.VMEM((sums, own, width), BF16),
            pltpu.SemaphoreType.DMA((core_slots, CHUNKS)),
            pltpu.SemaphoreType.DMA((core_slots, CHUNKS)),
            pltpu.SemaphoreType.DMA((side_slots, CHUNKS)),
            pltpu.SemaphoreType.DMA((side_slots, CHUNKS)),
        ],
        compiler_params=pltpu.CompilerParams(
            collective_id=number, has_side_effects=True, vmem_limit_bytes=VMEM_LIMIT
        ),
        name=name,
    )(*parts, *extra)


def middle_step(chunk, rows, here, totals, extra, outs):
    tokens, gain = extra
    _, middle = outs
    value = tokens[rows, :].astype(F32) + totals[0]
    middle[here, :] = value
    hat, _ = norm_parts(value)
    return (hat * gain[...]).astype(BF16)


def middle_back_step(chunk, rows, here, totals, extra, outs):
    middle, gain, cotangent = extra
    _, grad_middle, grad_gain = outs
    hat, inverse = norm_parts(middle[here, :])
    value = cotangent[here, :].astype(F32) + norm_back(hat, inverse, gain[...], totals[0])
    grad_middle[here, :] = value
    term = jnp.sum(totals[0] * hat, axis=0, keepdims=True)
    if chunk == 0:
        grad_gain[...] = term
    else:
        grad_gain[...] += term
    return value.astype(BF16)


def last_step(chunk, rows, here, totals, extra, outs):
    tokens, gain, middle, grad_middle = extra
    grad_tokens, block_out = outs
    hat, inverse = norm_parts(tokens[rows, :].astype(F32))
    grad_tokens[here, :] = grad_middle[here, :] + norm_back(hat, inverse, gain[...], totals[0])
    block_out[here, :] = (middle[here, :] + totals[1]).astype(BF16)
    return None


def group_sum_kernel(part, total, arrived, send_sem, recv_sem):
    me = lax.axis_index("tensor")
    barrier = pltpu.get_barrier_semaphore()
    for hop in range(1, 4):
        pl.semaphore_signal(
            barrier,
            inc=1,
            device_id={"tensor": (me + hop) % 4},
            device_id_type=pl.DeviceIdType.MESH,
        )
    pl.semaphore_wait(barrier, 3)
    copies = []
    for hop in range(1, 4):
        copy = pltpu.make_async_remote_copy(
            src_ref=part,
            dst_ref=arrived.at[hop - 1],
            send_sem=send_sem.at[hop - 1],
            recv_sem=recv_sem.at[hop - 1],
            device_id={"tensor": (me + hop) % 4},
            device_id_type=pl.DeviceIdType.MESH,
        )
        copy.start()
        copies.append(copy)
    for copy in copies:
        copy.wait()
    value = jnp.zeros(part.shape, F32)
    for owner in range(4):
        hop = (me - owner + 4) % 4
        term = jnp.where(hop == 0, part[...], 0.0)
        for slot in range(3):
            term = term + jnp.where(hop == slot + 1, arrived[slot], 0.0)
        value = value + term
    total[...] = value


def group_sum(part):
    return pl.pallas_call(
        group_sum_kernel,
        in_specs=[VMEM],
        out_specs=VMEM,
        out_shape=jax.ShapeDtypeStruct(part.shape, F32),
        scratch_shapes=[
            pltpu.VMEM((3,) + part.shape, F32),
            pltpu.SemaphoreType.DMA((3,)),
            pltpu.SemaphoreType.DMA((3,)),
        ],
        compiler_params=pltpu.CompilerParams(collective_id=4, has_side_effects=True),
        name="group_sum",
    )(part)


def half_turn(array):
    columns = array.reshape(array.shape[0], -1, 2, HEAD_DIM // 2)
    return np.stack([-columns[:, :, 1], columns[:, :, 0]], axis=2).reshape(array.shape)


def turn_matrix(width):
    return jnp.asarray(half_turn(np.eye(width, dtype=np.float32)), BF16)


def rotary_tables(rows, heads):
    half_width = HEAD_DIM // 2
    frequency = THETA ** (-(jnp.arange(half_width, dtype=F32) * 2.0 / HEAD_DIM))
    angles = jnp.arange(SEQ_LEN, dtype=F32)[:, None] * frequency[None, :]
    angles = jnp.tile(angles, (1, 2 * heads))
    repeat = rows // SEQ_LEN
    return jnp.tile(jnp.cos(angles), (repeat, 1)), jnp.tile(jnp.sin(angles), (repeat, 1))


def on_device(
    tokens,
    first_gain,
    joint_weight,
    output_weight,
    second_gain,
    expand_weight,
    shrink_weight,
    cotangent,
):
    local_rows, model_width = tokens.shape
    own_rows = cotangent.shape[0]
    heads = joint_weight.shape[2] // HEAD_DIM
    inner = heads * HEAD_DIM
    units = expand_weight.shape[2]
    joint_flat = joint_weight.reshape(model_width, 3 * inner)
    expand_flat = expand_weight.reshape(model_width, 2 * units)
    gain_one_row = first_gain.reshape(1, model_width)
    gain_two_row = second_gain.reshape(1, model_width)
    turn = turn_matrix(inner)

    grad_rows = lax.all_gather(cotangent, "tensor", axis=0, tiled=True)

    first_hat, _ = norm_parts(tokens.astype(F32))
    normed = (first_hat * first_gain).astype(BF16)
    turned = [dot(joint_weight[:, part], turn).astype(BF16) for part in (0, 1)]
    joint = dot(normed, jnp.concatenate([joint_flat, *turned], axis=1))
    cosine, sine = rotary_tables(local_rows, heads)
    query = (joint[:, :inner] * cosine + joint[:, 3 * inner : 4 * inner] * sine).astype(BF16)
    key = (joint[:, inner : 2 * inner] * cosine + joint[:, 4 * inner :] * sine).astype(BF16)
    value = joint[:, 2 * inner : 3 * inner].astype(BF16)
    query_t, key_t, value_t = query.T, key.T, value.T
    mixed_t, logsum = attend(key, query_t, value_t, heads, 256)
    branch_part = dot(mixed_t, output_weight, ((0,), (0,))).astype(BF16)
    second, middle = exchange(
        "middle_exchange",
        1,
        [branch_part],
        [tokens, gain_two_row],
        middle_step,
        True,
        [
            jax.ShapeDtypeStruct((local_rows, model_width), BF16),
            jax.ShapeDtypeStruct((own_rows, model_width), F32),
        ],
    )
    gate_up = dot(second, expand_flat)

    def activate(gate_part, up_part):
        return jax.nn.gelu(gate_part, approximate=True) * up_part

    hidden, activate_back = jax.vjp(activate, gate_up[:, :units], gate_up[:, units:])
    hidden = hidden.astype(BF16)
    grad_hidden = dot(grad_rows, shrink_weight, ((1,), (1,)))
    grad_gate, grad_up = activate_back(grad_hidden)
    grad_both = jnp.concatenate([grad_gate, grad_up], axis=1).astype(BF16)
    second_part = dot(grad_both, expand_flat, ((1,), (1,))).astype(BF16)
    grad_branch, grad_middle, gain_two = exchange(
        "middle_back_exchange",
        2,
        [second_part],
        [middle, gain_two_row, cotangent],
        middle_back_step,
        True,
        [
            jax.ShapeDtypeStruct((local_rows, model_width), BF16),
            jax.ShapeDtypeStruct((own_rows, model_width), F32),
            jax.ShapeDtypeStruct((1, model_width), F32),
        ],
    )
    grad_shrink = dot(hidden, grad_rows, ((0,), (0,))).astype(BF16)
    grad_expand = dot(second, grad_both, ((0,), (0,))).astype(BF16)
    grad_shrink, grad_expand = lax.psum((grad_shrink, grad_expand), "dp")

    grad_mixed = dot(grad_branch, output_weight, ((1,), (1,))).astype(BF16)
    dq_t, dk, dv = attend_back(
        key, key_t, query, query_t, value, grad_mixed, grad_mixed.T, logsum, heads, 256
    )

    def turn_back(grad):
        return grad * cosine + dot((grad * sine).astype(BF16), turn, ((1,), (1,)))

    grad_joint = jnp.concatenate([turn_back(dq_t.T), turn_back(dk), dv], axis=1).astype(BF16)
    first_part = dot(grad_joint, joint_flat, ((1,), (1,)))
    gain_one = jnp.sum(first_part * first_hat, axis=0, keepdims=True)
    grad_joint_w = dot(normed, grad_joint, ((0,), (0,))).astype(BF16)
    grad_output = dot(mixed_t, grad_branch).astype(BF16)
    gains = jnp.concatenate([gain_one, gain_two], axis=0).astype(BF16)
    grad_joint_w, grad_output, gains, grad_shrink, grad_expand = lax.optimization_barrier(
        (grad_joint_w, grad_output, gains, grad_shrink, grad_expand)
    )
    grad_joint_w, grad_output, gains = lax.psum((grad_joint_w, grad_output, gains), "dp")

    shrink_part = dot(hidden, shrink_weight).astype(BF16)
    grad_tokens, block_out = exchange(
        "last_exchange",
        3,
        [first_part.astype(BF16), shrink_part],
        [tokens, gain_one_row, middle, grad_middle],
        last_step,
        False,
        [
            jax.ShapeDtypeStruct((own_rows, model_width), F32),
            jax.ShapeDtypeStruct((own_rows, model_width), BF16),
        ],
    )
    gains = group_sum(gains.astype(F32))
    return (
        block_out,
        grad_tokens,
        gains[0],
        grad_joint_w.astype(F32).reshape(model_width, 3, inner),
        grad_output.astype(F32),
        gains[1],
        grad_expand.astype(F32).reshape(model_width, 2, units),
        grad_shrink.astype(F32),
    )


def solution(mesh):
    return jax.shard_map(
        on_device,
        mesh=mesh,
        in_specs=(
            P("dp", None),
            P(),
            P(None, None, "tensor"),
            P("tensor", None),
            P(),
            P(None, None, "tensor"),
            P("tensor", None),
            P(("dp", "tensor"), None),
        ),
        out_specs=(
            P(("dp", "tensor"), None),
            P(("dp", "tensor"), None),
            P(),
            P(None, None, "tensor"),
            P("tensor", None),
            P(),
            P(None, None, "tensor"),
            P("tensor", None),
        ),
        check_vma=False,
    )
```

```python
import functools

import jax
import jax.numpy as jnp
import numpy as np
from jax import lax
from jax.experimental import pallas as pl
from jax.experimental.pallas import tpu as pltpu
from jax.sharding import PartitionSpec as P

HEAD_DIM = 64
SEQ_LEN = 1024
EPS = 1e-05
THETA = 160000.0
SCALE = HEAD_DIM**-0.5
CHUNKS = 2
WAVES = 2
VMEM_LIMIT = 48 * 1024 * 1024
F32 = jnp.float32
BF16 = jnp.bfloat16
VMEM = pl.BlockSpec(memory_space=pltpu.VMEM)


def dot(a, b, dims=((1,), (0,))):
    return lax.dot_general(a, b, (dims, ((), ())), preferred_element_type=F32)


def norm_parts(values):
    centred = values - jnp.mean(values, axis=-1, keepdims=True)
    inverse = lax.rsqrt(jnp.mean(centred * centred, axis=-1, keepdims=True) + EPS)
    return centred * inverse, inverse


def norm_back(hat, inverse, gain, grad):
    scaled = grad * gain
    return inverse * (
        scaled
        - jnp.mean(scaled, axis=-1, keepdims=True)
        - hat * jnp.mean(scaled * hat, axis=-1, keepdims=True)
    )


def head_rows(array, head):
    index = lax.broadcasted_iota(jnp.int32, array.shape, 0) // HEAD_DIM
    return jnp.where(index == head, array, jnp.zeros_like(array))


def head_columns(array, head):
    index = lax.broadcasted_iota(jnp.int32, array.shape, 1) // HEAD_DIM
    return jnp.where(index == head, array, jnp.zeros_like(array))


def attend_kernel(heads, key, query_t, value_t, mixed_t, logsum):
    for head in range(heads):
        rows = slice(head * HEAD_DIM, (head + 1) * HEAD_DIM)
        scores = dot(key[...], head_rows(query_t[...], head))
        peak = jnp.max(scores, axis=0, keepdims=True)
        exps = jnp.exp(scores - peak)
        total = jnp.sum(exps, axis=0, keepdims=True)
        mixed_t[rows, :] = (dot(value_t[rows, :], exps.astype(BF16)) * (1.0 / total)).astype(BF16)
        logsum[head : head + 1, :] = peak + jnp.log(total)


def attend(key, query_t, value_t, heads, block):
    width, rows = query_t.shape
    per_seq = SEQ_LEN // block
    return pl.pallas_call(
        functools.partial(attend_kernel, heads),
        grid=(rows // block,),
        in_specs=[
            pl.BlockSpec((SEQ_LEN, width), lambda i: (i // per_seq, 0)),
            pl.BlockSpec((width, block), lambda i: (0, i)),
            pl.BlockSpec((width, SEQ_LEN), lambda i: (0, i // per_seq)),
        ],
        out_specs=[
            pl.BlockSpec((width, block), lambda i: (0, i)),
            pl.BlockSpec((8, block), lambda i: (0, i)),
        ],
        out_shape=[
            jax.ShapeDtypeStruct((width, rows), BF16),
            jax.ShapeDtypeStruct((8, rows), F32),
        ],
        compiler_params=pltpu.CompilerParams(vmem_limit_bytes=VMEM_LIMIT),
        name="attend",
    )(key, query_t, value_t)


def attend_back_kernel(
    heads, per_seq, key, key_t, query, query_t, value, grad, grad_t, mixed_t, logsum, dq_t, dk, dv
):
    @pl.when(pl.program_id(0) % per_seq == 0)
    def _():
        dk[...] = jnp.zeros_like(dk)
        dv[...] = jnp.zeros_like(dv)

    for head in range(heads):
        rows = slice(head * HEAD_DIM, (head + 1) * HEAD_DIM)
        scores = dot(key[...], head_rows(query_t[...], head))
        probs = jnp.exp(scores - logsum[head : head + 1, :])
        dprobs = dot(value[...], head_rows(grad_t[...], head))
        delta = jnp.sum(
            grad_t[rows, :].astype(F32) * mixed_t[rows, :].astype(F32), axis=0, keepdims=True
        )
        dscores = (probs * (dprobs - delta)).astype(BF16)
        dq_t[rows, :] = dot(key_t[rows, :], dscores) * SCALE
        dk[...] += dot(dscores, head_columns(query[...], head))
        dv[...] += dot(probs.astype(BF16), head_columns(grad[...], head))


def attend_back(key, key_t, query, query_t, value, grad, grad_t, mixed_t, logsum, heads, block):
    width, rows = query_t.shape
    per_seq = SEQ_LEN // block
    seq_down = pl.BlockSpec((SEQ_LEN, width), lambda i: (i // per_seq, 0))
    seq_across = pl.BlockSpec((width, SEQ_LEN), lambda i: (0, i // per_seq))
    down = pl.BlockSpec((block, width), lambda i: (i, 0))
    across = pl.BlockSpec((width, block), lambda i: (0, i))
    return pl.pallas_call(
        functools.partial(attend_back_kernel, heads, per_seq),
        grid=(rows // block,),
        in_specs=[
            seq_down,
            seq_across,
            down,
            across,
            seq_down,
            down,
            across,
            across,
            pl.BlockSpec((8, block), lambda i: (0, i)),
        ],
        out_specs=[across, seq_down, seq_down],
        out_shape=[
            jax.ShapeDtypeStruct((width, rows), F32),
            jax.ShapeDtypeStruct((rows, width), F32),
            jax.ShapeDtypeStruct((rows, width), F32),
        ],
        compiler_params=pltpu.CompilerParams(vmem_limit_bytes=VMEM_LIMIT),
        cost_estimate=pl.CostEstimate(
            flops=16 * rows * SEQ_LEN * width, bytes_accessed=16 * rows * width, transcendentals=0
        ),
        name="attend_back",
    )(key, key_t, query, query_t, value, grad, grad_t, mixed_t, logsum)


def remote(src, dst, send_sem, recv_sem, target):
    copy = pltpu.make_async_remote_copy(
        src_ref=src,
        dst_ref=dst,
        send_sem=send_sem,
        recv_sem=recv_sem,
        device_id=target,
        device_id_type=pl.DeviceIdType.MESH,
    )
    copy.start()
    return copy


def greet(targets):
    barrier = pltpu.get_barrier_semaphore()
    for target in targets:
        pl.semaphore_signal(
            barrier, inc=1, device_id=target, device_id_type=pl.DeviceIdType.MESH
        )
    pl.semaphore_wait(barrier, len(targets))


class GroupSum:
    def __init__(self, parts, own, gather, scratch):
        self.parts, self.own, self.gather = parts, own, gather
        self.from_core, self.to_side, self.from_side = scratch[:3]
        self.core_send, self.core_recv, self.side_send, self.side_recv = scratch[3:]
        me = lax.axis_index("tensor")
        side, core = me // 2, me % 2
        self.me = me
        self.core_peer = side * 2 + (1 - core)
        self.side_peer = (1 - side) * 2 + core
        self.cross = (1 - side) * 2 + (1 - core)
        self.rows = own // CHUNKS
        self.unsent = []

    def peers(self):
        return [{"tensor": self.core_peer}, {"tensor": self.side_peer}]

    def at(self, owner, chunk):
        return pl.ds(pl.multiple_of(owner * self.own + chunk * self.rows, 16), self.rows)

    def here(self, chunk):
        return pl.ds(chunk * self.rows, self.rows)

    def to_core(self, src, dst, slot, chunk):
        sems = self.core_send.at[slot, chunk], self.core_recv.at[slot, chunk]
        copy = remote(src, dst, *sems, {"tensor": self.core_peer})
        self.unsent.append(copy)
        return copy

    def over(self, src, dst, slot, chunk):
        sems = self.side_send.at[slot, chunk], self.side_recv.at[slot, chunk]
        copy = remote(src, dst, *sems, {"tensor": self.side_peer})
        self.unsent.append(copy)
        return copy

    def start(self):
        self.onward, self.mine, self.sideways = {}, {}, {}
        for first, kept, owner in ((0, self.onward, self.cross), (1, self.mine, self.core_peer)):
            for slot, part in enumerate(self.parts):
                for chunk in range(CHUNKS):
                    kept[slot, chunk] = self.to_core(
                        part.at[self.at(owner, chunk)],
                        self.from_core.at[2 * slot + first, self.here(chunk)],
                        2 * slot + first,
                        chunk,
                    )

    def cross_over(self):
        for slot, part in enumerate(self.parts):
            for chunk in range(CHUNKS):
                here = self.here(chunk)
                self.onward[slot, chunk].wait_recv()
                self.to_side[slot, here] = (
                    part[self.at(self.side_peer, chunk)].astype(F32)
                    + self.from_core[2 * slot, here].astype(F32)
                ).astype(BF16)
                self.sideways[slot, chunk] = self.over(
                    self.to_side.at[slot, here], self.from_side.at[slot, here], slot, chunk
                )

    def total(self, slot, chunk):
        here = self.here(chunk)
        self.mine[slot, chunk].wait_recv()
        self.sideways[slot, chunk].wait_recv()
        return (
            self.parts[slot][self.at(self.me, chunk)].astype(F32)
            + self.from_core[2 * slot + 1, here].astype(F32)
            + self.from_side[slot, here].astype(F32)
        )

    def finish(self, step, extra, outs):
        sums = len(self.parts)
        gathered = []
        for chunk in range(CHUNKS):
            totals = [self.total(slot, chunk) for slot in range(sums)]
            result = step(chunk, self.at(self.me, chunk), self.here(chunk), totals, extra, outs)
            if self.gather:
                outs[0][self.at(self.me, chunk), :] = result
                block = outs[0].at[self.at(self.me, chunk)]
                over = self.over(block, block, sums, chunk)
                gathered.append((over, self.to_core(block, block, 2 * sums, chunk)))
        relayed = []
        for chunk, (over, _) in enumerate(gathered):
            over.wait_recv()
            block = outs[0].at[self.at(self.side_peer, chunk)]
            relayed.append(self.to_core(block, block, 2 * sums + 1, chunk))
        for _, near in gathered:
            near.wait_recv()
        for relay in relayed:
            relay.wait_recv()

    def close(self):
        for copy in self.unsent:
            copy.wait_send()


def exchange_kernel(sums, extras, step, own, *refs):
    work = GroupSum(refs[:sums], own, True, refs[-7:])
    greet(work.peers())
    work.start()
    work.cross_over()
    work.finish(step, refs[sums : sums + extras], refs[sums + extras : -7])
    work.close()


def exchange_scratch(sums, own, width, gather):
    core_slots = 2 * sums + (2 if gather else 0)
    side_slots = sums + (1 if gather else 0)
    return [
        pltpu.VMEM((2 * sums, own, width), BF16),
        pltpu.VMEM((sums, own, width), BF16),
        pltpu.VMEM((sums, own, width), BF16),
        pltpu.SemaphoreType.DMA((core_slots, CHUNKS)),
        pltpu.SemaphoreType.DMA((core_slots, CHUNKS)),
        pltpu.SemaphoreType.DMA((side_slots, CHUNKS)),
        pltpu.SemaphoreType.DMA((side_slots, CHUNKS)),
    ]


def exchange(name, number, parts, extra, step, out_shape):
    own = parts[0].shape[0] // 4
    sums = len(parts)
    return pl.pallas_call(
        functools.partial(exchange_kernel, sums, len(extra), step, own),
        in_specs=[VMEM] * (sums + len(extra)),
        out_specs=[VMEM] * len(out_shape),
        out_shape=out_shape,
        scratch_shapes=exchange_scratch(sums, own, parts[0].shape[1], True),
        compiler_params=pltpu.CompilerParams(
            collective_id=number, has_side_effects=True, vmem_limit_bytes=VMEM_LIMIT
        ),
        name=name,
    )(*parts, *extra)


def middle_step(chunk, rows, here, totals, extra, outs):
    tokens, gain = extra
    _, middle = outs
    value = tokens[rows, :].astype(F32) + totals[0]
    middle[here, :] = value
    hat, _ = norm_parts(value)
    return (hat * gain[...]).astype(BF16)


def middle_back_step(chunk, rows, here, totals, extra, outs):
    middle, gain, cotangent = extra
    _, grad_middle, grad_gain = outs
    hat, inverse = norm_parts(middle[here, :])
    value = cotangent[here, :].astype(F32) + norm_back(hat, inverse, gain[...], totals[0])
    grad_middle[here, :] = value
    term = jnp.sum(totals[0] * hat, axis=0, keepdims=True)
    if chunk == 0:
        grad_gain[...] = term
    else:
        grad_gain[...] += term
    return value.astype(BF16)


def last_step(chunk, rows, here, totals, extra, outs):
    tokens, gain, middle, grad_middle = extra
    grad_tokens, block_out = outs
    hat, inverse = norm_parts(tokens[rows, :].astype(F32))
    grad_tokens[here, :] = grad_middle[here, :] + norm_back(hat, inverse, gain[...], totals[0])
    block_out[here, :] = (middle[here, :] + totals[1]).astype(BF16)
    return None


class DataSum:
    def __init__(self, payload, total, scratch):
        self.payload, self.result = payload, total
        self.from_pair, self.summed, self.arrived = scratch[:3]
        self.pair_send, self.pair_recv, self.far_send, self.far_recv = scratch[3:]
        self.waves, _, self.count = payload.shape[:3]
        data = lax.axis_index("dp")
        self.outer, self.inner = data // 2, data % 2
        self.unsent = []

    def pair(self):
        return {"dp": self.outer * 2 + (1 - self.inner)}

    def far(self, hop):
        return {"dp": (self.outer + hop) % self.count * 2 + self.inner}

    def peers(self):
        return [self.pair()] + [self.far(hop) for hop in range(1, self.count)]

    def place(self, hop):
        return (self.outer + hop) % self.count

    def behind(self, hop):
        return (self.outer + self.count - hop) % self.count

    def to_pair(self, src, dst, *sem):
        copy = remote(src, dst, self.pair_send.at[sem], self.pair_recv.at[sem], self.pair())
        self.unsent.append(copy)
        return copy

    def to_far(self, src, dst, hop, *sem):
        copy = remote(src, dst, self.far_send.at[sem], self.far_recv.at[sem], self.far(hop))
        self.unsent.append(copy)
        return copy

    def hops(self):
        return [*range(1, self.count), 0]

    def start(self):
        self.near = {
            (wave, hop): self.to_pair(
                self.payload.at[wave, 1 - self.inner, self.place(hop)],
                self.from_pair.at[wave, hop],
                0,
                wave,
                hop,
            )
            for wave in range(self.waves)
            for hop in self.hops()
        }
        self.spread = {}
        self.shared = {}

    def scatter(self, wave):
        for hop in self.hops():
            self.near[wave, hop].wait_recv()
            self.summed[wave, hop] = (
                self.payload[wave, self.inner, self.place(hop)].astype(F32)
                + self.from_pair[wave, hop].astype(F32)
            ).astype(BF16)
            if hop:
                self.spread[wave, hop] = self.to_far(
                    self.summed.at[wave, hop], self.arrived.at[wave, hop - 1], hop, 0, wave, hop
                )

    def collect(self, wave):
        value = self.summed[wave, 0].astype(F32)
        for hop in range(1, self.count):
            self.spread[wave, hop].wait_recv()
            value = value + self.arrived[wave, hop - 1].astype(F32)
        self.result[wave, self.inner, self.outer] = value.astype(BF16)
        block = self.result.at[wave, self.inner, self.outer]
        for hop in range(1, self.count):
            self.shared[wave, hop] = self.to_far(block, block, hop, 1, wave, hop)
        self.shared[wave, 0] = self.to_pair(block, block, 1, wave, 0)

    def relay(self, wave):
        for hop in range(1, self.count):
            self.shared[wave, hop].wait_recv()
            block = self.result.at[wave, self.inner, self.behind(hop)]
            self.near[wave, hop] = self.to_pair(block, block, 1, wave, hop)

    def finish(self):
        for wave in range(self.waves):
            self.shared[wave, 0].wait_recv()
            for hop in range(1, self.count):
                self.near[wave, hop].wait_recv()

    def close(self):
        for copy in self.unsent:
            copy.wait_send()


class GainSum:
    def __init__(self, terms, total, group, data, scratch):
        self.terms, self.total, self.group, self.data = terms, total, group, data
        self.held, self.paired, self.outer = scratch[:3]
        self.send, self.recv = scratch[3:]
        self.unsent = []

    def copy(self, src, dst, target, sem):
        copy = remote(src, dst, self.send.at[sem], self.recv.at[sem], target)
        self.unsent.append(copy)
        return copy

    def start(self):
        me = self.group.me
        self.held[me] = self.terms[...]
        self.first = [
            self.copy(self.held.at[me], self.held.at[me], {"tensor": (me + hop) % 4}, hop - 1)
            for hop in range(1, 4)
        ]

    def pair_up(self):
        for copy in self.first:
            copy.wait_recv()
        self.paired[0] = (self.held[0] + self.held[1]) + (self.held[2] + self.held[3])
        self.second = self.copy(self.paired.at[0], self.paired.at[1], self.data.pair(), 3)

    def spread(self):
        self.second.wait_recv()
        outer = self.data.outer
        self.outer[outer] = self.paired[0] + self.paired[1]
        self.third = [
            self.copy(self.outer.at[outer], self.outer.at[outer], self.data.far(hop), 3 + hop)
            for hop in range(1, self.data.count)
        ]

    def finish(self):
        for copy in self.third:
            copy.wait_recv()
        value = self.outer[0]
        for number in range(1, self.data.count):
            value = value + self.outer[number]
        self.total[...] = value

    def close(self):
        for copy in self.unsent:
            copy.wait_send()


def last_kernel(own, *refs):
    first_part, shrink_part, payload, terms, *extra = refs[:8]
    grad_tokens, block_out, summed, gains = refs[8:12]
    scratch = refs[12:]
    group = GroupSum((first_part, shrink_part), own, False, scratch[:7])
    data = DataSum(payload, summed, scratch[7:14])
    gain = GainSum(terms, gains, group, data, scratch[14:])
    greet(group.peers() + [{"tensor": group.cross}] + data.peers())
    data.start()
    gain.start()
    group.start()
    group.cross_over()
    gain.pair_up()
    for wave in range(data.waves):
        data.scatter(wave)
        if wave:
            data.collect(wave - 1)
    data.collect(data.waves - 1)
    gain.spread()
    group.finish(last_step, extra, (grad_tokens, block_out))
    for wave in range(data.waves):
        data.relay(wave)
    gain.finish()
    data.finish()
    for work in (group, data, gain):
        work.close()


def last_exchange(first_part, shrink_part, payload, terms, *extra):
    own, width = first_part.shape[0] // 4, first_part.shape[1]
    waves, _, count, rows, _ = payload.shape
    pieces = (waves, count, rows, width)
    return pl.pallas_call(
        functools.partial(last_kernel, own),
        in_specs=[VMEM] * 8,
        out_specs=[VMEM] * 4,
        out_shape=[
            jax.ShapeDtypeStruct((own, width), F32),
            jax.ShapeDtypeStruct((own, width), BF16),
            jax.ShapeDtypeStruct(payload.shape, BF16),
            jax.ShapeDtypeStruct(terms.shape, F32),
        ],
        scratch_shapes=[
            *exchange_scratch(2, own, width, False),
            pltpu.VMEM(pieces, BF16),
            pltpu.VMEM(pieces, BF16),
            pltpu.VMEM(pieces, BF16),
            pltpu.SemaphoreType.DMA((2, waves, count)),
            pltpu.SemaphoreType.DMA((2, waves, count)),
            pltpu.SemaphoreType.DMA((2, waves, count)),
            pltpu.SemaphoreType.DMA((2, waves, count)),
            pltpu.VMEM((4,) + terms.shape, F32),
            pltpu.VMEM((2,) + terms.shape, F32),
            pltpu.VMEM((count,) + terms.shape, F32),
            pltpu.SemaphoreType.DMA((3 + count,)),
            pltpu.SemaphoreType.DMA((3 + count,)),
        ],
        compiler_params=pltpu.CompilerParams(
            collective_id=3, has_side_effects=True, vmem_limit_bytes=VMEM_LIMIT
        ),
        name="last_exchange",
    )(first_part, shrink_part, payload, terms, *extra)


def to_payload(rows):
    count, width = lax.axis_size("dp") // 2, rows.shape[1]
    piece = -(-rows.shape[0] // (WAVES * 2 * count * 16)) * 16
    padding = WAVES * 2 * count * piece - rows.shape[0]
    return jnp.pad(rows, ((0, padding), (0, 0))).reshape(WAVES, 2, count, piece, width)


def half_turn(array):
    columns = array.reshape(array.shape[0], -1, 2, HEAD_DIM // 2)
    return np.stack([-columns[:, :, 1], columns[:, :, 0]], axis=2).reshape(array.shape)


def turn_matrix(width):
    return jnp.asarray(half_turn(np.eye(width, dtype=np.float32)), BF16)


def rotary_tables(rows, heads):
    half_width = HEAD_DIM // 2
    frequency = THETA ** (-(jnp.arange(half_width, dtype=F32) * 2.0 / HEAD_DIM))
    angles = jnp.arange(SEQ_LEN, dtype=F32)[:, None] * frequency[None, :]
    angles = jnp.tile(angles, (1, 2 * heads))
    repeat = rows // SEQ_LEN
    return jnp.tile(jnp.cos(angles), (repeat, 1)), jnp.tile(jnp.sin(angles), (repeat, 1))


def on_device(
    tokens,
    first_gain,
    joint_weight,
    output_weight,
    second_gain,
    expand_weight,
    shrink_weight,
    cotangent,
):
    local_rows, model_width = tokens.shape
    own_rows = cotangent.shape[0]
    heads = joint_weight.shape[2] // HEAD_DIM
    inner = heads * HEAD_DIM
    units = expand_weight.shape[2]
    joint_flat = joint_weight.reshape(model_width, 3 * inner)
    expand_flat = expand_weight.reshape(model_width, 2 * units)
    gain_one_row = first_gain.reshape(1, model_width)
    gain_two_row = second_gain.reshape(1, model_width)
    turn = turn_matrix(inner)

    grad_rows = lax.all_gather(cotangent, "tensor", axis=0, tiled=True)

    first_hat, _ = norm_parts(tokens.astype(F32))
    normed = (first_hat * first_gain).astype(BF16)
    turned = [dot(joint_weight[:, part], turn).astype(BF16) for part in (0, 1)]
    joint = dot(normed, jnp.concatenate([joint_flat, *turned], axis=1))
    cosine, sine = rotary_tables(local_rows, heads)
    query = (joint[:, :inner] * cosine + joint[:, 3 * inner : 4 * inner] * sine).astype(BF16)
    query = query * jnp.asarray(SCALE, BF16)
    key = (joint[:, inner : 2 * inner] * cosine + joint[:, 4 * inner :] * sine).astype(BF16)
    value = joint[:, 2 * inner : 3 * inner].astype(BF16)
    query_t, key_t, value_t = query.T, key.T, value.T
    mixed_t, logsum = attend(key, query_t, value_t, heads, 256)
    branch_part = dot(mixed_t, output_weight, ((0,), (0,))).astype(BF16)
    second, middle = exchange(
        "middle_exchange",
        1,
        [branch_part],
        [tokens, gain_two_row],
        middle_step,
        [
            jax.ShapeDtypeStruct((local_rows, model_width), BF16),
            jax.ShapeDtypeStruct((own_rows, model_width), F32),
        ],
    )
    gate_up = dot(second, expand_flat)

    def activate(gate_part, up_part):
        return jax.nn.gelu(gate_part, approximate=True) * up_part

    hidden, activate_back = jax.vjp(activate, gate_up[:, :units], gate_up[:, units:])
    hidden = hidden.astype(BF16)
    grad_hidden = dot(grad_rows, shrink_weight, ((1,), (1,)))
    grad_gate, grad_up = activate_back(grad_hidden)
    grad_both = jnp.concatenate([grad_gate, grad_up], axis=1).astype(BF16)
    second_part = dot(grad_both, expand_flat, ((1,), (1,))).astype(BF16)
    grad_shrink = dot(hidden, grad_rows, ((0,), (0,))).astype(BF16)
    grad_expand = dot(second, grad_both, ((0,), (0,))).astype(BF16)
    second_part, grad_shrink, grad_expand = lax.optimization_barrier(
        (second_part, grad_shrink, grad_expand)
    )
    grad_shrink, grad_expand = lax.psum((grad_shrink, grad_expand), "dp")
    grad_branch, grad_middle, gain_two = exchange(
        "middle_back_exchange",
        2,
        [second_part],
        [middle, gain_two_row, cotangent],
        middle_back_step,
        [
            jax.ShapeDtypeStruct((local_rows, model_width), BF16),
            jax.ShapeDtypeStruct((own_rows, model_width), F32),
            jax.ShapeDtypeStruct((1, model_width), F32),
        ],
    )
    grad_mixed = dot(grad_branch, output_weight, ((1,), (1,))).astype(BF16)
    dq_t, dk, dv = attend_back(
        key, key_t, query, query_t, value, grad_mixed, grad_mixed.T, mixed_t, logsum, heads, 256
    )

    def turn_back(grad):
        return grad * cosine + dot((grad * sine).astype(BF16), turn, ((1,), (1,)))

    grad_joint = jnp.concatenate([turn_back(dq_t.T), turn_back(dk), dv], axis=1).astype(BF16)
    first_part = dot(grad_joint, joint_flat, ((1,), (1,)))
    gain_one = jnp.sum(first_part * first_hat, axis=0, keepdims=True)
    grad_joint_w = dot(grad_joint, normed, ((0,), (0,)))
    grad_output = dot(mixed_t, grad_branch)
    weights = jnp.concatenate([grad_joint_w, grad_output], axis=0).astype(BF16)
    gains = jnp.concatenate([gain_one, gain_two, jnp.zeros((6, model_width), F32)], axis=0)
    shrink_part = dot(hidden, shrink_weight).astype(BF16)
    grad_tokens, block_out, weights, gains = last_exchange(
        first_part.astype(BF16),
        shrink_part,
        to_payload(weights),
        gains,
        tokens,
        gain_one_row,
        middle,
        grad_middle,
    )
    weights = weights.reshape(-1, model_width)
    grad_joint_w = weights[: 3 * inner].astype(F32).T
    return (
        block_out,
        grad_tokens,
        gains[0],
        grad_joint_w.reshape(model_width, 3, inner),
        weights[3 * inner : 4 * inner].astype(F32),
        gains[1],
        grad_expand.astype(F32).reshape(model_width, 2, units),
        grad_shrink.astype(F32),
    )


def solution(mesh):
    return jax.shard_map(
        on_device,
        mesh=mesh,
        in_specs=(
            P("dp", None),
            P(),
            P(None, None, "tensor"),
            P("tensor", None),
            P(),
            P(None, None, "tensor"),
            P("tensor", None),
            P(("dp", "tensor"), None),
        ),
        out_specs=(
            P(("dp", "tensor"), None),
            P(("dp", "tensor"), None),
            P(),
            P(None, None, "tensor"),
            P("tensor", None),
            P(),
            P(None, None, "tensor"),
            P("tensor", None),
        ),
        check_vma=False,
    )
```

```python
import functools

import jax
import jax.numpy as jnp
import numpy as np
from jax import lax
from jax.experimental import pallas as pl
from jax.experimental.pallas import tpu as pltpu
from jax.sharding import PartitionSpec as P

HEAD_DIM = 64
SEQ_LEN = 1024
EPS = 1e-05
THETA = 160000.0
SCALE = HEAD_DIM**-0.5
CHUNKS = 2
WAVES = 2
VMEM_LIMIT = 48 * 1024 * 1024
F32 = jnp.float32
BF16 = jnp.bfloat16
VMEM = pl.BlockSpec(memory_space=pltpu.VMEM)


def dot(a, b, dims=((1,), (0,))):
    return lax.dot_general(a, b, (dims, ((), ())), preferred_element_type=F32)


def norm_parts(values):
    centred = values - jnp.mean(values, axis=-1, keepdims=True)
    inverse = lax.rsqrt(jnp.mean(centred * centred, axis=-1, keepdims=True) + EPS)
    return centred * inverse, inverse


def norm_back(hat, inverse, gain, grad):
    scaled = grad * gain
    return inverse * (
        scaled
        - jnp.mean(scaled, axis=-1, keepdims=True)
        - hat * jnp.mean(scaled * hat, axis=-1, keepdims=True)
    )


def head_rows(array, head):
    index = lax.broadcasted_iota(jnp.int32, array.shape, 0) // HEAD_DIM
    return jnp.where(index == head, array, jnp.zeros_like(array))


def head_columns(array, head):
    index = lax.broadcasted_iota(jnp.int32, array.shape, 1) // HEAD_DIM
    return jnp.where(index == head, array, jnp.zeros_like(array))


def attend_kernel(heads, key, query_t, value_t, mixed_t, logsum):
    for head in range(heads):
        rows = slice(head * HEAD_DIM, (head + 1) * HEAD_DIM)
        scores = dot(key[...], head_rows(query_t[...], head))
        peak = jnp.max(scores, axis=0, keepdims=True)
        exps = jnp.exp(scores - peak)
        total = jnp.sum(exps, axis=0, keepdims=True)
        mixed_t[rows, :] = (dot(value_t[rows, :], exps.astype(BF16)) * (1.0 / total)).astype(BF16)
        logsum[head : head + 1, :] = peak + jnp.log(total)


def attend(key, query_t, value_t, heads, block):
    width, rows = query_t.shape
    per_seq = SEQ_LEN // block
    return pl.pallas_call(
        functools.partial(attend_kernel, heads),
        grid=(rows // block,),
        in_specs=[
            pl.BlockSpec((SEQ_LEN, width), lambda i: (i // per_seq, 0)),
            pl.BlockSpec((width, block), lambda i: (0, i)),
            pl.BlockSpec((width, SEQ_LEN), lambda i: (0, i // per_seq)),
        ],
        out_specs=[
            pl.BlockSpec((width, block), lambda i: (0, i)),
            pl.BlockSpec((8, block), lambda i: (0, i)),
        ],
        out_shape=[
            jax.ShapeDtypeStruct((width, rows), BF16),
            jax.ShapeDtypeStruct((8, rows), F32),
        ],
        compiler_params=pltpu.CompilerParams(vmem_limit_bytes=VMEM_LIMIT),
        name="attend",
    )(key, query_t, value_t)


def remote(src, dst, send_sem, recv_sem, target):
    copy = pltpu.make_async_remote_copy(
        src_ref=src,
        dst_ref=dst,
        send_sem=send_sem,
        recv_sem=recv_sem,
        device_id=target,
        device_id_type=pl.DeviceIdType.MESH,
    )
    copy.start()
    return copy


def greet(targets):
    barrier = pltpu.get_barrier_semaphore()
    for target in targets:
        pl.semaphore_signal(
            barrier, inc=1, device_id=target, device_id_type=pl.DeviceIdType.MESH
        )
    pl.semaphore_wait(barrier, len(targets))


class GroupSum:
    def __init__(self, parts, own, gather, scratch):
        self.parts, self.own, self.gather = parts, own, gather
        self.from_core, self.to_side, self.from_side = scratch[:3]
        self.core_send, self.core_recv, self.side_send, self.side_recv = scratch[3:]
        me = lax.axis_index("tensor")
        side, core = me // 2, me % 2
        self.me = me
        self.core_peer = side * 2 + (1 - core)
        self.side_peer = (1 - side) * 2 + core
        self.cross = (1 - side) * 2 + (1 - core)
        self.rows = own // CHUNKS
        self.unsent = []

    def peers(self):
        return [{"tensor": self.core_peer}, {"tensor": self.side_peer}]

    def at(self, owner, chunk):
        return pl.ds(pl.multiple_of(owner * self.own + chunk * self.rows, 16), self.rows)

    def here(self, chunk):
        return pl.ds(chunk * self.rows, self.rows)

    def to_core(self, src, dst, slot, chunk):
        sems = self.core_send.at[slot, chunk], self.core_recv.at[slot, chunk]
        copy = remote(src, dst, *sems, {"tensor": self.core_peer})
        self.unsent.append(copy)
        return copy

    def over(self, src, dst, slot, chunk):
        sems = self.side_send.at[slot, chunk], self.side_recv.at[slot, chunk]
        copy = remote(src, dst, *sems, {"tensor": self.side_peer})
        self.unsent.append(copy)
        return copy

    def start(self):
        self.onward, self.mine, self.sideways = {}, {}, {}
        for first, kept, owner in ((0, self.onward, self.cross), (1, self.mine, self.core_peer)):
            for slot, part in enumerate(self.parts):
                for chunk in range(CHUNKS):
                    kept[slot, chunk] = self.to_core(
                        part.at[self.at(owner, chunk)],
                        self.from_core.at[2 * slot + first, self.here(chunk)],
                        2 * slot + first,
                        chunk,
                    )

    def cross_over(self):
        for slot, part in enumerate(self.parts):
            for chunk in range(CHUNKS):
                here = self.here(chunk)
                self.onward[slot, chunk].wait_recv()
                self.to_side[slot, here] = (
                    part[self.at(self.side_peer, chunk)].astype(F32)
                    + self.from_core[2 * slot, here].astype(F32)
                ).astype(BF16)
                self.sideways[slot, chunk] = self.over(
                    self.to_side.at[slot, here], self.from_side.at[slot, here], slot, chunk
                )

    def total(self, slot, chunk):
        here = self.here(chunk)
        self.mine[slot, chunk].wait_recv()
        self.sideways[slot, chunk].wait_recv()
        return (
            self.parts[slot][self.at(self.me, chunk)].astype(F32)
            + self.from_core[2 * slot + 1, here].astype(F32)
            + self.from_side[slot, here].astype(F32)
        )

    def totals(self, step, extra, outs):
        sums = len(self.parts)
        self.gathered = []
        for chunk in range(CHUNKS):
            totals = [self.total(slot, chunk) for slot in range(sums)]
            result = step(chunk, self.at(self.me, chunk), self.here(chunk), totals, extra, outs)
            if self.gather:
                outs[0][self.at(self.me, chunk), :] = result
                block = outs[0].at[self.at(self.me, chunk)]
                over = self.over(block, block, sums, chunk)
                near = self.to_core(block, block, 2 * sums, chunk)
                self.gathered.append((over, near))

    def spread(self, whole):
        sums = len(self.parts)
        relayed = []
        for chunk, (over, _) in enumerate(self.gathered):
            over.wait_recv()
            block = whole.at[self.at(self.side_peer, chunk)]
            relayed.append(self.to_core(block, block, 2 * sums + 1, chunk))
        for _, near in self.gathered:
            near.wait_recv()
        for relay in relayed:
            relay.wait_recv()

    def close(self):
        for copy in self.unsent:
            copy.wait_send()


def exchange_kernel(sums, extras, step, own, *refs):
    work = GroupSum(refs[:sums], own, True, refs[-7:])
    greet(work.peers())
    work.start()
    work.cross_over()
    outs = refs[sums + extras : -7]
    work.totals(step, refs[sums : sums + extras], outs)
    work.spread(outs[0])
    work.close()


def exchange_scratch(sums, own, width, gather):
    core_slots = 2 * sums + (2 if gather else 0)
    side_slots = sums + (1 if gather else 0)
    return [
        pltpu.VMEM((2 * sums, own, width), BF16),
        pltpu.VMEM((sums, own, width), BF16),
        pltpu.VMEM((sums, own, width), BF16),
        pltpu.SemaphoreType.DMA((core_slots, CHUNKS)),
        pltpu.SemaphoreType.DMA((core_slots, CHUNKS)),
        pltpu.SemaphoreType.DMA((side_slots, CHUNKS)),
        pltpu.SemaphoreType.DMA((side_slots, CHUNKS)),
    ]


def exchange(name, number, parts, extra, step, out_shape):
    own = parts[0].shape[0] // 4
    sums = len(parts)
    return pl.pallas_call(
        functools.partial(exchange_kernel, sums, len(extra), step, own),
        in_specs=[VMEM] * (sums + len(extra)),
        out_specs=[VMEM] * len(out_shape),
        out_shape=out_shape,
        scratch_shapes=exchange_scratch(sums, own, parts[0].shape[1], True),
        compiler_params=pltpu.CompilerParams(
            collective_id=number, has_side_effects=True, vmem_limit_bytes=VMEM_LIMIT
        ),
        name=name,
    )(*parts, *extra)


def middle_step(chunk, rows, here, totals, extra, outs):
    tokens, gain = extra
    _, middle = outs
    value = tokens[rows, :].astype(F32) + totals[0]
    middle[here, :] = value
    hat, _ = norm_parts(value)
    return (hat * gain[...]).astype(BF16)


def middle_back_step(chunk, rows, here, totals, extra, outs):
    middle, gain, cotangent = extra
    _, grad_middle, grad_gain = outs
    hat, inverse = norm_parts(middle[here, :])
    value = cotangent[here, :].astype(F32) + norm_back(hat, inverse, gain[...], totals[0])
    grad_middle[here, :] = value
    term = jnp.sum(totals[0] * hat, axis=0, keepdims=True)
    if chunk == 0:
        grad_gain[...] = term
    else:
        grad_gain[...] += term
    return value.astype(BF16)


def token_step(chunk, rows, here, totals, extra, outs):
    tokens, gain, grad_middle = extra
    hat, inverse = norm_parts(tokens[rows, :].astype(F32))
    outs[0][here, :] = grad_middle[here, :] + norm_back(hat, inverse, gain[...], totals[0])


def out_step(chunk, rows, here, totals, extra, outs):
    outs[0][here, :] = (extra[0][here, :] + totals[0]).astype(BF16)


class DataSum:
    def __init__(self, payload, total, scratch):
        self.payload, self.result = payload, total
        self.from_pair, self.summed, self.arrived = scratch[:3]
        self.pair_send, self.pair_recv, self.far_send, self.far_recv = scratch[3:]
        self.waves, self.count = WAVES, payload.shape[0] // (2 * WAVES)
        data = lax.axis_index("dp")
        self.outer, self.inner = data // 2, data % 2
        self.unsent = []

    def pair(self):
        return {"dp": self.outer * 2 + (1 - self.inner)}

    def far(self, hop):
        return {"dp": (self.outer + hop) % self.count * 2 + self.inner}

    def peers(self):
        return [self.pair()] + [self.far(hop) for hop in range(1, self.count)]

    def unit(self, wave, inner, outer):
        return (wave * 2 + inner) * self.count + outer

    def place(self, hop):
        return (self.outer + hop) % self.count

    def behind(self, hop):
        return (self.outer + self.count - hop) % self.count

    def to_pair(self, src, dst, *sem):
        copy = remote(src, dst, self.pair_send.at[sem], self.pair_recv.at[sem], self.pair())
        self.unsent.append(copy)
        return copy

    def to_far(self, src, dst, hop, *sem):
        copy = remote(src, dst, self.far_send.at[sem], self.far_recv.at[sem], self.far(hop))
        self.unsent.append(copy)
        return copy

    def hops(self):
        return [*range(1, self.count), 0]

    def start(self):
        self.near = {
            (wave, hop): self.to_pair(
                self.payload.at[self.unit(wave, 1 - self.inner, self.place(hop))],
                self.from_pair.at[wave, hop],
                0,
                wave,
                hop,
            )
            for wave in range(self.waves)
            for hop in self.hops()
        }
        self.spread = {}
        self.shared = {}

    def scatter(self, wave):
        for hop in self.hops():
            self.near[wave, hop].wait_recv()
            self.summed[wave, hop] = (
                self.payload[self.unit(wave, self.inner, self.place(hop))].astype(F32)
                + self.from_pair[wave, hop].astype(F32)
            ).astype(BF16)
            if hop:
                self.spread[wave, hop] = self.to_far(
                    self.summed.at[wave, hop], self.arrived.at[wave, hop - 1], hop, 0, wave, hop
                )

    def collect(self, wave):
        value = self.summed[wave, 0].astype(F32)
        for hop in range(1, self.count):
            self.spread[wave, hop].wait_recv()
            value = value + self.arrived[wave, hop - 1].astype(F32)
        self.result[self.unit(wave, self.inner, self.outer)] = value.astype(BF16)
        block = self.result.at[self.unit(wave, self.inner, self.outer)]
        for hop in range(1, self.count):
            self.shared[wave, hop] = self.to_far(block, block, hop, 1, wave, hop)
        self.shared[wave, 0] = self.to_pair(block, block, 1, wave, 0)

    def relay(self, wave):
        for hop in range(1, self.count):
            self.shared[wave, hop].wait_recv()
            block = self.result.at[self.unit(wave, self.inner, self.behind(hop))]
            self.near[wave, hop] = self.to_pair(block, block, 1, wave, hop)

    def finish(self):
        for wave in range(self.waves):
            self.shared[wave, 0].wait_recv()
            for hop in range(1, self.count):
                self.near[wave, hop].wait_recv()

    def close(self):
        for copy in self.unsent:
            copy.wait_send()


class GainSum:
    def __init__(self, terms, total, group, data, scratch):
        self.terms, self.total, self.group, self.data = terms, total, group, data
        self.held, self.paired, self.outer = scratch[:3]
        self.send, self.recv = scratch[3:]
        self.unsent = []

    def copy(self, src, dst, target, sem):
        copy = remote(src, dst, self.send.at[sem], self.recv.at[sem], target)
        self.unsent.append(copy)
        return copy

    def start(self):
        me = self.group.me
        self.held[me] = self.terms[...]
        self.first = [
            self.copy(self.held.at[me], self.held.at[me], {"tensor": (me + hop) % 4}, hop - 1)
            for hop in range(1, 4)
        ]

    def pair_up(self):
        for copy in self.first:
            copy.wait_recv()
        self.paired[0] = (self.held[0] + self.held[1]) + (self.held[2] + self.held[3])
        self.second = self.copy(self.paired.at[0], self.paired.at[1], self.data.pair(), 3)

    def spread(self):
        self.second.wait_recv()
        outer = self.data.outer
        self.outer[outer] = self.paired[0] + self.paired[1]
        self.third = [
            self.copy(self.outer.at[outer], self.outer.at[outer], self.data.far(hop), 3 + hop)
            for hop in range(1, self.data.count)
        ]

    def finish(self):
        for copy in self.third:
            copy.wait_recv()
        value = self.outer[0]
        for number in range(1, self.data.count):
            value = value + self.outer[number]
        self.total[...] = value

    def close(self):
        for copy in self.unsent:
            copy.wait_send()


def back_kernel(heads, own, count, *refs):
    (
        second_part,
        shrink_part,
        early_part,
        tokens,
        gain_one,
        gain_two,
        middle,
        cotangent,
        output_weight,
        joint,
        normed,
        cosine,
        sine,
        turn,
        key,
        key_t,
        query,
        query_t,
        value,
        mixed_t,
        logsum,
    ) = refs[:21]
    block_out, grad_tokens, early_sum, late_sum, gains = refs[21:26]
    grad_branch, grad_middle, term_two, first_part, late_part, terms = refs[26:32]
    grad_mixed, grad_mixed_t, dq_t, dk, dv = refs[32:37]
    scratch = refs[37:]
    rows, width = tokens.shape
    inner = heads * HEAD_DIM
    block = 256

    norm_sum = GroupSum((second_part,), own, True, scratch[:7])
    out_sum = GroupSum((shrink_part,), own, False, scratch[7:14])
    token_sum = GroupSum((first_part,), own, False, scratch[14:21])
    early = DataSum(early_part, early_sum, scratch[21:28])
    late = DataSum(late_part, late_sum, scratch[28:35])
    gain = GainSum(terms, gains, norm_sum, early, scratch[35:40])
    greet(norm_sum.peers() + [{"tensor": norm_sum.cross}] + early.peers())

    norm_sum.start()
    early.start()
    norm_sum.cross_over()
    early.scatter(0)
    norm_sum.totals(
        middle_back_step,
        (middle, gain_two, cotangent),
        (grad_branch, grad_middle, term_two),
    )
    early.scatter(1)
    early.collect(0)
    norm_sum.spread(grad_branch)
    out_sum.start()
    early.collect(1)

    grad_mixed[...] = dot(grad_branch[...], output_weight[...], ((1,), (1,))).astype(BF16)
    grad_mixed_t[...] = dot(output_weight[...], grad_branch[...], ((1,), (1,))).astype(BF16)
    dk[...] = jnp.zeros_like(dk)
    dv[...] = jnp.zeros_like(dv)

    def attend_rows(number, carry):
        down = pl.ds(pl.multiple_of(number * block, block), block)
        for head in range(heads):
            part = slice(head * HEAD_DIM, (head + 1) * HEAD_DIM)
            scores = dot(key[...], head_rows(query_t[:, down], head))
            probs = jnp.exp(scores - logsum[head : head + 1, down])
            grad_t = grad_mixed_t[:, down]
            dprobs = dot(value[...], head_rows(grad_t, head))
            delta = jnp.sum(
                grad_mixed_t[part, down].astype(F32) * mixed_t[part, down].astype(F32),
                axis=0,
                keepdims=True,
            )
            dscores = (probs * (dprobs - delta)).astype(BF16)
            dq_t[part, down] = dot(key_t[part, :], dscores) * SCALE
            dk[...] += dot(dscores, head_columns(query[down, :], head))
            dv[...] += dot(probs.astype(BF16), head_columns(grad_mixed[down, :], head))
        return carry

    blocks = rows // block
    lax.fori_loop(0, blocks // 2, attend_rows, 0)
    out_sum.cross_over()
    early.relay(0)
    lax.fori_loop(blocks // 2, blocks, attend_rows, 0)
    early.relay(1)

    def turn_back(grad):
        moved = dot((grad * sine[...]).astype(BF16), turn[...], ((1,), (1,)))
        return (grad * cosine[...] + moved).astype(BF16)

    grad_parts = (turn_back(dq_t[...].T[:, :inner]), turn_back(dk[...]), dv[...].astype(BF16))
    gain_term = jnp.zeros((1, width), F32)
    for owner in range(rows // own):
        here = slice(owner * own, (owner + 1) * own)
        value_rows = sum(
            dot(grad_parts[part][here], joint[part], ((1,), (1,))) for part in range(3)
        )
        first_part[here, :] = value_rows.astype(BF16)
        gain_term += jnp.sum(value_rows * normed[here, :].astype(F32), axis=0, keepdims=True)
    token_sum.start()
    terms[...] = jnp.zeros_like(terms)
    terms[0:1, :] = gain_term / gain_one[...]
    terms[1:2, :] = term_two[...]
    gain.start()

    units, piece, _ = late_part.shape
    step = inner // piece
    for part in range(3):
        grad_weight = dot(grad_parts[part], normed[...], ((0,), (0,))).astype(BF16)
        late_part[part * step : (part + 1) * step] = grad_weight.reshape(step, piece, width)
    grad_output = dot(mixed_t[...], grad_branch[...]).astype(BF16)
    late_part[3 * step : 4 * step] = grad_output.reshape(step, piece, width)
    if units > 4 * step:
        late_part[4 * step :] = jnp.zeros((units - 4 * step, piece, width), BF16)
    late.start()
    token_sum.cross_over()
    gain.pair_up()
    out_sum.totals(out_step, (middle,), (block_out,))
    early.finish()
    late.scatter(0)
    late.scatter(1)
    late.collect(0)
    gain.spread()
    late.collect(1)
    token_sum.totals(token_step, (tokens, gain_one, grad_middle), (grad_tokens,))
    late.relay(0)
    late.relay(1)
    gain.finish()
    late.finish()
    for work in (norm_sum, out_sum, token_sum, early, late, gain):
        work.close()


def sum_scratch(units, piece, width, count):
    held = pltpu.VMEM((WAVES, count, piece, width), BF16)
    return [held] * 3 + [pltpu.SemaphoreType.DMA((2, WAVES, count))] * 4


def piece_rows(rows, count):
    return -(-rows // (WAVES * 2 * count * 16)) * 16


def back(second_part, shrink_part, early_part, *rest, heads, own):
    rows, width = second_part.shape
    count = lax.axis_size("dp") // 2
    inner = heads * HEAD_DIM
    early_shape = early_part.shape
    late_shape = (WAVES * 2 * count, piece_rows(4 * inner, count), width)
    padded = -(-inner // 128) * 128
    return pl.pallas_call(
        functools.partial(back_kernel, heads, own, count),
        in_specs=[VMEM] * 21,
        out_specs=[VMEM] * 5,
        out_shape=[
            jax.ShapeDtypeStruct((own, width), BF16),
            jax.ShapeDtypeStruct((own, width), F32),
            jax.ShapeDtypeStruct(early_shape, BF16),
            jax.ShapeDtypeStruct(late_shape, BF16),
            jax.ShapeDtypeStruct((8, width), F32),
        ],
        scratch_shapes=[
            pltpu.VMEM((rows, width), BF16),
            pltpu.VMEM((own, width), F32),
            pltpu.VMEM((1, width), F32),
            pltpu.VMEM((rows, width), BF16),
            pltpu.VMEM(late_shape, BF16),
            pltpu.VMEM((8, width), F32),
            pltpu.VMEM((rows, inner), BF16),
            pltpu.VMEM((inner, rows), BF16),
            pltpu.VMEM((padded, rows), F32),
            pltpu.VMEM((rows, inner), F32),
            pltpu.VMEM((rows, inner), F32),
            *exchange_scratch(1, own, width, True),
            *exchange_scratch(1, own, width, False),
            *exchange_scratch(1, own, width, False),
            *sum_scratch(*early_shape, count),
            *sum_scratch(*late_shape, count),
            pltpu.VMEM((4, 8, width), F32),
            pltpu.VMEM((2, 8, width), F32),
            pltpu.VMEM((count, 8, width), F32),
            pltpu.SemaphoreType.DMA((3 + count,)),
            pltpu.SemaphoreType.DMA((3 + count,)),
        ],
        compiler_params=pltpu.CompilerParams(
            collective_id=3, has_side_effects=True, vmem_limit_bytes=56 * 1024 * 1024
        ),
        name="back",
    )(second_part, shrink_part, early_part, *rest)


def to_payload(rows):
    count, width = lax.axis_size("dp") // 2, rows.shape[1]
    piece = piece_rows(rows.shape[0], count)
    units = WAVES * 2 * count
    padding = units * piece - rows.shape[0]
    return jnp.pad(rows, ((0, padding), (0, 0))).reshape(units, piece, width)


def half_turn(array):
    columns = array.reshape(array.shape[0], -1, 2, HEAD_DIM // 2)
    return np.stack([-columns[:, :, 1], columns[:, :, 0]], axis=2).reshape(array.shape)


def turn_matrix(width):
    return jnp.asarray(half_turn(np.eye(width, dtype=np.float32)), BF16)


def rotary_tables(rows, heads):
    half_width = HEAD_DIM // 2
    frequency = THETA ** (-(jnp.arange(half_width, dtype=F32) * 2.0 / HEAD_DIM))
    angles = jnp.arange(SEQ_LEN, dtype=F32)[:, None] * frequency[None, :]
    angles = jnp.tile(angles, (1, 2 * heads))
    repeat = rows // SEQ_LEN
    return jnp.tile(jnp.cos(angles), (repeat, 1)), jnp.tile(jnp.sin(angles), (repeat, 1))


def on_device(
    tokens,
    first_gain,
    joint_weight,
    output_weight,
    second_gain,
    expand_weight,
    shrink_weight,
    cotangent,
):
    local_rows, model_width = tokens.shape
    own_rows = cotangent.shape[0]
    heads = joint_weight.shape[2] // HEAD_DIM
    inner = heads * HEAD_DIM
    units = expand_weight.shape[2]
    joint_flat = joint_weight.reshape(model_width, 3 * inner)
    expand_flat = expand_weight.reshape(model_width, 2 * units)
    gain_one_row = first_gain.reshape(1, model_width)
    gain_two_row = second_gain.reshape(1, model_width)
    turn = turn_matrix(inner)

    grad_rows = lax.all_gather(cotangent, "tensor", axis=0, tiled=True)

    first_hat, _ = norm_parts(tokens.astype(F32))
    normed = (first_hat * first_gain).astype(BF16)
    turned = [dot(joint_weight[:, part], turn).astype(BF16) for part in (0, 1)]
    joint = dot(normed, jnp.concatenate([joint_flat, *turned], axis=1))
    cosine, sine = rotary_tables(local_rows, heads)
    query = (joint[:, :inner] * cosine + joint[:, 3 * inner : 4 * inner] * sine).astype(BF16)
    query = query * jnp.asarray(SCALE, BF16)
    key = (joint[:, inner : 2 * inner] * cosine + joint[:, 4 * inner :] * sine).astype(BF16)
    value = joint[:, 2 * inner : 3 * inner].astype(BF16)
    query_t, key_t, value_t = query.T, key.T, value.T
    mixed_t, logsum = attend(key, query_t, value_t, heads, 256)
    branch_part = dot(mixed_t, output_weight, ((0,), (0,))).astype(BF16)
    second, middle = exchange(
        "middle_exchange",
        1,
        [branch_part],
        [tokens, gain_two_row],
        middle_step,
        [
            jax.ShapeDtypeStruct((local_rows, model_width), BF16),
            jax.ShapeDtypeStruct((own_rows, model_width), F32),
        ],
    )
    gate_up = dot(second, expand_flat)

    def activate(gate_part, up_part):
        return jax.nn.gelu(gate_part, approximate=True) * up_part

    hidden, activate_back = jax.vjp(activate, gate_up[:, :units], gate_up[:, units:])
    hidden = hidden.astype(BF16)
    grad_hidden = dot(grad_rows, shrink_weight, ((1,), (1,)))
    grad_gate, grad_up = activate_back(grad_hidden)
    grad_both = jnp.concatenate([grad_gate, grad_up], axis=1).astype(BF16)
    second_part = dot(grad_both, expand_flat, ((1,), (1,))).astype(BF16)
    grad_shrink = dot(hidden, grad_rows, ((0,), (0,)))
    grad_expand = dot(grad_both, second, ((0,), (0,)))
    early = jnp.concatenate([grad_shrink, grad_expand], axis=0).astype(BF16)
    shrink_part = dot(hidden, shrink_weight).astype(BF16)
    block_out, grad_tokens, early, late, gains = back(
        second_part,
        shrink_part,
        to_payload(early),
        tokens,
        gain_one_row,
        gain_two_row,
        middle,
        cotangent,
        output_weight,
        jnp.transpose(joint_weight, (1, 0, 2)),
        normed,
        cosine,
        sine,
        turn,
        key,
        key_t,
        query,
        query_t,
        value,
        mixed_t,
        logsum,
        heads=heads,
        own=own_rows,
    )
    early = early.reshape(-1, model_width)
    late = late.reshape(-1, model_width)
    grad_joint_w = late[: 3 * inner].astype(F32).T
    grad_expand = early[units : 3 * units].astype(F32).T
    return (
        block_out,
        grad_tokens,
        gains[0],
        grad_joint_w.reshape(model_width, 3, inner),
        late[3 * inner : 4 * inner].astype(F32),
        gains[1],
        grad_expand.reshape(model_width, 2, units),
        early[:units].astype(F32),
    )


def solution(mesh):
    return jax.shard_map(
        on_device,
        mesh=mesh,
        in_specs=(
            P("dp", None),
            P(),
            P(None, None, "tensor"),
            P("tensor", None),
            P(),
            P(None, None, "tensor"),
            P("tensor", None),
            P(("dp", "tensor"), None),
        ),
        out_specs=(
            P(("dp", "tensor"), None),
            P(("dp", "tensor"), None),
            P(),
            P(None, None, "tensor"),
            P("tensor", None),
            P(),
            P(None, None, "tensor"),
            P("tensor", None),
        ),
        check_vma=False,
    )
```

```python
import functools

import jax
import jax.numpy as jnp
import numpy as np
from jax import lax
from jax.experimental import pallas as pl
from jax.experimental.pallas import tpu as pltpu
from jax.sharding import PartitionSpec as P

HEAD_DIM = 64
SEQ_LEN = 1024
EPS = 1e-05
THETA = 160000.0
SCALE = HEAD_DIM**-0.5
CHUNKS = 2
WAVES = 2
VMEM_LIMIT = 48 * 1024 * 1024
F32 = jnp.float32
BF16 = jnp.bfloat16
VMEM = pl.BlockSpec(memory_space=pltpu.VMEM)


def dot(a, b, dims=((1,), (0,))):
    return lax.dot_general(a, b, (dims, ((), ())), preferred_element_type=F32)


def norm_parts(values):
    centred = values - jnp.mean(values, axis=-1, keepdims=True)
    inverse = lax.rsqrt(jnp.mean(centred * centred, axis=-1, keepdims=True) + EPS)
    return centred * inverse, inverse


def norm_back(hat, inverse, gain, grad):
    scaled = grad * gain
    return inverse * (
        scaled
        - jnp.mean(scaled, axis=-1, keepdims=True)
        - hat * jnp.mean(scaled * hat, axis=-1, keepdims=True)
    )


def head_rows(array, head):
    index = lax.broadcasted_iota(jnp.int32, array.shape, 0) // HEAD_DIM
    return jnp.where(index == head, array, jnp.zeros_like(array))


def head_columns(array, head):
    index = lax.broadcasted_iota(jnp.int32, array.shape, 1) // HEAD_DIM
    return jnp.where(index == head, array, jnp.zeros_like(array))


def remote(src, dst, send_sem, recv_sem, target):
    copy = pltpu.make_async_remote_copy(
        src_ref=src,
        dst_ref=dst,
        send_sem=send_sem,
        recv_sem=recv_sem,
        device_id=target,
        device_id_type=pl.DeviceIdType.MESH,
    )
    copy.start()
    return copy


def greet(targets):
    barrier = pltpu.get_barrier_semaphore()
    for target in targets:
        pl.semaphore_signal(
            barrier, inc=1, device_id=target, device_id_type=pl.DeviceIdType.MESH
        )
    pl.semaphore_wait(barrier, len(targets))


class GroupSum:
    def __init__(self, parts, own, gather, scratch):
        self.parts, self.own, self.gather = parts, own, gather
        self.from_core, self.to_side, self.from_side = scratch[:3]
        self.core_send, self.core_recv, self.side_send, self.side_recv = scratch[3:]
        me = lax.axis_index("tensor")
        side, core = me // 2, me % 2
        self.me = me
        self.core_peer = side * 2 + (1 - core)
        self.side_peer = (1 - side) * 2 + core
        self.cross = (1 - side) * 2 + (1 - core)
        self.rows = own // CHUNKS
        self.unsent = []

    def peers(self):
        return [{"tensor": self.core_peer}, {"tensor": self.side_peer}]

    def at(self, owner, chunk):
        return pl.ds(pl.multiple_of(owner * self.own + chunk * self.rows, 16), self.rows)

    def here(self, chunk):
        return pl.ds(chunk * self.rows, self.rows)

    def to_core(self, src, dst, slot, chunk):
        sems = self.core_send.at[slot, chunk], self.core_recv.at[slot, chunk]
        copy = remote(src, dst, *sems, {"tensor": self.core_peer})
        self.unsent.append(copy)
        return copy

    def over(self, src, dst, slot, chunk):
        sems = self.side_send.at[slot, chunk], self.side_recv.at[slot, chunk]
        copy = remote(src, dst, *sems, {"tensor": self.side_peer})
        self.unsent.append(copy)
        return copy

    def start(self):
        self.start_onward()
        self.start_mine()

    def start_onward(self):
        self.onward = self.send_block(0, self.cross)

    def start_mine(self):
        self.mine = self.send_block(1, self.core_peer)

    def send_block(self, first, owner):
        return {
            (slot, chunk): self.to_core(
                part.at[self.at(owner, chunk)],
                self.from_core.at[2 * slot + first, self.here(chunk)],
                2 * slot + first,
                chunk,
            )
            for slot, part in enumerate(self.parts)
            for chunk in range(CHUNKS)
        }

    def cross_over(self):
        self.sideways = {}
        for slot, part in enumerate(self.parts):
            for chunk in range(CHUNKS):
                here = self.here(chunk)
                self.onward[slot, chunk].wait_recv()
                self.to_side[slot, here] = (
                    part[self.at(self.side_peer, chunk)].astype(F32)
                    + self.from_core[2 * slot, here].astype(F32)
                ).astype(BF16)
                self.sideways[slot, chunk] = self.over(
                    self.to_side.at[slot, here], self.from_side.at[slot, here], slot, chunk
                )

    def total(self, slot, chunk):
        here = self.here(chunk)
        self.mine[slot, chunk].wait_recv()
        self.sideways[slot, chunk].wait_recv()
        return (
            self.parts[slot][self.at(self.me, chunk)].astype(F32)
            + self.from_core[2 * slot + 1, here].astype(F32)
            + self.from_side[slot, here].astype(F32)
        )

    def totals(self, step, extra, outs):
        sums = len(self.parts)
        self.gathered = []
        for chunk in range(CHUNKS):
            totals = [self.total(slot, chunk) for slot in range(sums)]
            result = step(chunk, self.at(self.me, chunk), self.here(chunk), totals, extra, outs)
            if self.gather:
                outs[0][self.at(self.me, chunk), :] = result
                block = outs[0].at[self.at(self.me, chunk)]
                over = self.over(block, block, sums, chunk)
                near = self.to_core(block, block, 2 * sums, chunk)
                self.gathered.append((over, near))

    def spread(self, whole):
        sums = len(self.parts)
        relayed = []
        for chunk, (over, _) in enumerate(self.gathered):
            over.wait_recv()
            block = whole.at[self.at(self.side_peer, chunk)]
            relayed.append(self.to_core(block, block, 2 * sums + 1, chunk))
        for _, near in self.gathered:
            near.wait_recv()
        for relay in relayed:
            relay.wait_recv()

    def close(self):
        for copy in self.unsent:
            copy.wait_send()


def exchange_scratch(sums, own, width, gather):
    core_slots = 2 * sums + (2 if gather else 0)
    side_slots = sums + (1 if gather else 0)
    return [
        pltpu.VMEM((2 * sums, own, width), BF16),
        pltpu.VMEM((sums, own, width), BF16),
        pltpu.VMEM((sums, own, width), BF16),
        pltpu.SemaphoreType.DMA((core_slots, CHUNKS)),
        pltpu.SemaphoreType.DMA((core_slots, CHUNKS)),
        pltpu.SemaphoreType.DMA((side_slots, CHUNKS)),
        pltpu.SemaphoreType.DMA((side_slots, CHUNKS)),
    ]


def front_kernel(heads, own, *refs):
    tokens, gain_one, gain_two, joint, output_weight, cosine, sine = refs[:7]
    second, middle, normed, key, key_t, query, query_t, value, mixed_t, logsum = refs[7:17]
    value_t, branch_part = refs[17:19]
    group = GroupSum((branch_part,), own, True, refs[19:])
    greet(group.peers())
    rows = tokens.shape[0]

    def project(number, carry):
        down = pl.ds(pl.multiple_of(number * own, own), own)
        hat, _ = norm_parts(tokens[down, :].astype(F32))
        normal = (hat * gain_one[...]).astype(BF16)
        normed[down, :] = normal
        cos, sin = cosine[down, :], sine[down, :]
        turned = (dot(normal, joint[0]) * cos + dot(normal, joint[3]) * sin) * SCALE
        query[down, :] = turned.astype(BF16)
        query_t[:, down] = turned.T.astype(BF16)
        turned = dot(normal, joint[1]) * cos + dot(normal, joint[4]) * sin
        key[down, :] = turned.astype(BF16)
        key_t[:, down] = turned.T.astype(BF16)
        plain = dot(normal, joint[2])
        value[down, :] = plain.astype(BF16)
        value_t[:, down] = plain.T.astype(BF16)
        return carry

    lax.fori_loop(0, rows // own, project, 0)

    def attend(owner):
        down = pl.ds(pl.multiple_of(owner * own, own), own)
        for head in range(heads):
            part = slice(head * HEAD_DIM, (head + 1) * HEAD_DIM)
            scores = dot(key[...], head_rows(query_t[:, down], head))
            peak = jnp.max(scores, axis=0, keepdims=True)
            exps = jnp.exp(scores - peak)
            total = jnp.sum(exps, axis=0, keepdims=True)
            mixed = dot(value_t[part, :], exps.astype(BF16)) * (1.0 / total)
            mixed_t[part, down] = mixed.astype(BF16)
            logsum[head : head + 1, down] = peak + jnp.log(total)
        branch = dot(mixed_t[:, down], output_weight[...], ((0,), (0,)))
        branch_part[down, :] = branch.astype(BF16)

    attend(group.cross)
    group.start_onward()
    attend(group.side_peer)
    group.cross_over()
    attend(group.core_peer)
    group.start_mine()
    attend(group.me)
    group.totals(middle_step, (tokens, gain_two), (second, middle))
    group.spread(second)
    group.close()


def front(tokens, *rest, heads, own):
    rows, width = tokens.shape
    inner = heads * HEAD_DIM
    down, across = (rows, inner), (inner, rows)
    shapes = [
        ((rows, width), BF16),
        ((own, width), F32),
        ((rows, width), BF16),
        (down, BF16),
        (across, BF16),
        (down, BF16),
        (across, BF16),
        (down, BF16),
        (across, BF16),
        ((8, rows), F32),
    ]
    return pl.pallas_call(
        functools.partial(front_kernel, heads, own),
        in_specs=[VMEM] * 7,
        out_specs=[VMEM] * 10,
        out_shape=[jax.ShapeDtypeStruct(*shape) for shape in shapes],
        scratch_shapes=[
            pltpu.VMEM(across, BF16),
            pltpu.VMEM((rows, width), BF16),
            *exchange_scratch(1, own, width, True),
        ],
        compiler_params=pltpu.CompilerParams(
            collective_id=1, has_side_effects=True, vmem_limit_bytes=VMEM_LIMIT
        ),
        name="front",
    )(tokens, *rest)


def middle_step(chunk, rows, here, totals, extra, outs):
    tokens, gain = extra
    _, middle = outs
    value = tokens[rows, :].astype(F32) + totals[0]
    middle[here, :] = value
    hat, _ = norm_parts(value)
    return (hat * gain[...]).astype(BF16)


def middle_back_step(chunk, rows, here, totals, extra, outs):
    middle, gain, cotangent = extra
    _, grad_middle, grad_gain = outs
    hat, inverse = norm_parts(middle[here, :])
    value = cotangent[here, :].astype(F32) + norm_back(hat, inverse, gain[...], totals[0])
    grad_middle[here, :] = value
    term = jnp.sum(totals[0] * hat, axis=0, keepdims=True)
    if chunk == 0:
        grad_gain[...] = term
    else:
        grad_gain[...] += term
    return value.astype(BF16)


def token_step(chunk, rows, here, totals, extra, outs):
    tokens, gain, grad_middle = extra
    hat, inverse = norm_parts(tokens[rows, :].astype(F32))
    outs[0][here, :] = grad_middle[here, :] + norm_back(hat, inverse, gain[...], totals[0])


def out_step(chunk, rows, here, totals, extra, outs):
    outs[0][here, :] = (extra[0][here, :] + totals[0]).astype(BF16)


class DataSum:
    def __init__(self, payload, total, scratch):
        self.payload, self.result = payload, total
        self.from_pair, self.summed, self.arrived = scratch[:3]
        self.pair_send, self.pair_recv, self.far_send, self.far_recv = scratch[3:]
        self.waves, self.count = WAVES, payload.shape[0] // (2 * WAVES)
        data = lax.axis_index("dp")
        self.outer, self.inner = data // 2, data % 2
        self.near, self.spread, self.shared = {}, {}, {}
        self.unsent = []

    def pair(self):
        return {"dp": self.outer * 2 + (1 - self.inner)}

    def far(self, hop):
        return {"dp": (self.outer + hop) % self.count * 2 + self.inner}

    def peers(self):
        return [self.pair()] + [self.far(hop) for hop in range(1, self.count)]

    def unit(self, wave, inner, outer):
        return (wave * 2 + inner) * self.count + outer

    def place(self, hop):
        return (self.outer + hop) % self.count

    def behind(self, hop):
        return (self.outer + self.count - hop) % self.count

    def to_pair(self, src, dst, *sem):
        copy = remote(src, dst, self.pair_send.at[sem], self.pair_recv.at[sem], self.pair())
        self.unsent.append(copy)
        return copy

    def to_far(self, src, dst, hop, *sem):
        copy = remote(src, dst, self.far_send.at[sem], self.far_recv.at[sem], self.far(hop))
        self.unsent.append(copy)
        return copy

    def hops(self):
        return [*range(1, self.count), 0]

    def start(self, wave):
        for hop in self.hops():
            self.near[wave, hop] = self.to_pair(
                self.payload.at[self.unit(wave, 1 - self.inner, self.place(hop))],
                self.from_pair.at[wave, hop],
                0,
                wave,
                hop,
            )

    def scatter(self, wave):
        for hop in self.hops():
            self.near[wave, hop].wait_recv()
            self.summed[wave, hop] = (
                self.payload[self.unit(wave, self.inner, self.place(hop))].astype(F32)
                + self.from_pair[wave, hop].astype(F32)
            ).astype(BF16)
            if hop:
                self.spread[wave, hop] = self.to_far(
                    self.summed.at[wave, hop], self.arrived.at[wave, hop - 1], hop, 0, wave, hop
                )

    def collect(self, wave):
        value = self.summed[wave, 0].astype(F32)
        for hop in range(1, self.count):
            self.spread[wave, hop].wait_recv()
            value = value + self.arrived[wave, hop - 1].astype(F32)
        self.result[self.unit(wave, self.inner, self.outer)] = value.astype(BF16)
        block = self.result.at[self.unit(wave, self.inner, self.outer)]
        for hop in range(1, self.count):
            self.shared[wave, hop] = self.to_far(block, block, hop, 1, wave, hop)
        self.shared[wave, 0] = self.to_pair(block, block, 1, wave, 0)

    def relay(self, wave):
        for hop in range(1, self.count):
            self.shared[wave, hop].wait_recv()
            block = self.result.at[self.unit(wave, self.inner, self.behind(hop))]
            self.near[wave, hop] = self.to_pair(block, block, 1, wave, hop)

    def finish(self):
        for wave in range(self.waves):
            self.shared[wave, 0].wait_recv()
            for hop in range(1, self.count):
                self.near[wave, hop].wait_recv()

    def close(self):
        for copy in self.unsent:
            copy.wait_send()


class GainSum:
    def __init__(self, terms, total, group, data, scratch):
        self.terms, self.total, self.group, self.data = terms, total, group, data
        self.held, self.paired, self.outer = scratch[:3]
        self.send, self.recv = scratch[3:]
        self.unsent = []

    def copy(self, src, dst, target, sem):
        copy = remote(src, dst, self.send.at[sem], self.recv.at[sem], target)
        self.unsent.append(copy)
        return copy

    def start(self):
        me = self.group.me
        self.held[me] = self.terms[...]
        self.first = [
            self.copy(self.held.at[me], self.held.at[me], {"tensor": (me + hop) % 4}, hop - 1)
            for hop in range(1, 4)
        ]

    def pair_up(self):
        for copy in self.first:
            copy.wait_recv()
        self.paired[0] = (self.held[0] + self.held[1]) + (self.held[2] + self.held[3])
        self.second = self.copy(self.paired.at[0], self.paired.at[1], self.data.pair(), 3)

    def spread(self):
        self.second.wait_recv()
        outer = self.data.outer
        self.outer[outer] = self.paired[0] + self.paired[1]
        self.third = [
            self.copy(self.outer.at[outer], self.outer.at[outer], self.data.far(hop), 3 + hop)
            for hop in range(1, self.data.count)
        ]

    def finish(self):
        for copy in self.third:
            copy.wait_recv()
        value = self.outer[0]
        for number in range(1, self.data.count):
            value = value + self.outer[number]
        self.total[...] = value

    def close(self):
        for copy in self.unsent:
            copy.wait_send()


def back_kernel(heads, own, count, *refs):
    (
        second_part,
        shrink_part,
        early_part,
        tokens,
        gain_one,
        gain_two,
        middle,
        cotangent,
        output_weight,
        joint,
        normed,
        cosine,
        sine,
        turn,
        key,
        key_t,
        query,
        query_t,
        value,
        mixed_t,
        logsum,
    ) = refs[:21]
    block_out, grad_tokens, early_sum, late_sum, gains = refs[21:26]
    grad_branch, grad_middle, term_two, first_part, late_part, terms = refs[26:32]
    grad_mixed, grad_mixed_t, dq_t, dk, dv = refs[32:37]
    scratch = refs[37:]
    rows, width = tokens.shape
    inner = heads * HEAD_DIM
    block = 256

    norm_sum = GroupSum((second_part,), own, True, scratch[:7])
    out_sum = GroupSum((shrink_part,), own, False, scratch[7:14])
    token_sum = GroupSum((first_part,), own, False, scratch[14:21])
    early = DataSum(early_part, early_sum, scratch[21:28])
    late = DataSum(late_part, late_sum, scratch[28:35])
    gain = GainSum(terms, gains, norm_sum, early, scratch[35:40])
    greet(norm_sum.peers() + [{"tensor": norm_sum.cross}] + early.peers())

    norm_sum.start()
    early.start(0)
    early.start(1)
    norm_sum.cross_over()
    early.scatter(0)
    norm_sum.totals(
        middle_back_step,
        (middle, gain_two, cotangent),
        (grad_branch, grad_middle, term_two),
    )
    early.scatter(1)
    early.collect(0)
    norm_sum.spread(grad_branch)
    out_sum.start()
    early.collect(1)

    late_step = inner // late_part.shape[1]
    grad_output = dot(mixed_t[...], grad_branch[...]).astype(BF16)
    late_part[:late_step] = grad_output.reshape((late_step,) + late_part.shape[1:])
    grad_mixed[...] = dot(grad_branch[...], output_weight[...], ((1,), (1,))).astype(BF16)
    grad_mixed_t[...] = dot(output_weight[...], grad_branch[...], ((1,), (1,))).astype(BF16)
    dk[...] = jnp.zeros_like(dk)
    dv[...] = jnp.zeros_like(dv)

    def attend_rows(number, carry):
        down = pl.ds(pl.multiple_of(number * block, block), block)
        for head in range(heads):
            part = slice(head * HEAD_DIM, (head + 1) * HEAD_DIM)
            scores = dot(key[...], head_rows(query_t[:, down], head))
            probs = jnp.exp(scores - logsum[head : head + 1, down])
            grad_t = grad_mixed_t[:, down]
            dprobs = dot(value[...], head_rows(grad_t, head))
            delta = jnp.sum(
                grad_mixed_t[part, down].astype(F32) * mixed_t[part, down].astype(F32),
                axis=0,
                keepdims=True,
            )
            dscores = (probs * (dprobs - delta)).astype(BF16)
            dq_t[part, down] = dot(key_t[part, :], dscores) * SCALE
            dk[...] += dot(dscores, head_columns(query[down, :], head))
            dv[...] += dot(probs.astype(BF16), head_columns(grad_mixed[down, :], head))
        return carry

    blocks = rows // block
    lax.fori_loop(0, blocks // 2, attend_rows, 0)
    out_sum.cross_over()
    early.relay(0)
    lax.fori_loop(blocks // 2, blocks, attend_rows, 0)
    early.relay(1)

    def turn_back(grad):
        moved = dot((grad * sine[...]).astype(BF16), turn[...], ((1,), (1,)))
        return (grad * cosine[...] + moved).astype(BF16)

    grad_parts = (turn_back(dq_t[...].T[:, :inner]), turn_back(dk[...]), dv[...].astype(BF16))
    units, piece, _ = late_part.shape
    step = inner // piece
    whole = units == 4 * step

    def keep(place, weight):
        kept = weight.astype(BF16).reshape(step, piece, width)
        late_part[place * step : (place + 1) * step] = kept

    if not whole:
        late_part[4 * step :] = jnp.zeros((units - 4 * step, piece, width), BF16)
    keep(1, dot(grad_parts[2], normed[...], ((0,), (0,))))
    if whole:
        late.start(0)
    keep(2, dot(grad_parts[0], normed[...], ((0,), (0,))))
    keep(3, dot(grad_parts[1], normed[...], ((0,), (0,))))
    if not whole:
        late.start(0)
    late.start(1)
    gain_term = jnp.zeros((1, width), F32)
    for owner in range(rows // own):
        here = slice(owner * own, (owner + 1) * own)
        value_rows = sum(
            dot(grad_parts[part][here], joint[part], ((1,), (1,))) for part in range(3)
        )
        first_part[here, :] = value_rows.astype(BF16)
        gain_term += jnp.sum(value_rows * normed[here, :].astype(F32), axis=0, keepdims=True)
    token_sum.start()
    terms[...] = jnp.zeros_like(terms)
    terms[0:1, :] = gain_term / gain_one[...]
    terms[1:2, :] = term_two[...]
    gain.start()
    late.scatter(0)
    token_sum.cross_over()
    gain.pair_up()
    late.scatter(1)
    late.collect(0)
    out_sum.totals(out_step, (middle,), (block_out,))
    gain.spread()
    late.collect(1)
    token_sum.totals(token_step, (tokens, gain_one, grad_middle), (grad_tokens,))
    late.relay(0)
    late.relay(1)
    gain.finish()
    early.finish()
    late.finish()
    for work in (norm_sum, out_sum, token_sum, early, late, gain):
        work.close()


def sum_scratch(units, piece, width, count):
    held = pltpu.VMEM((WAVES, count, piece, width), BF16)
    return [held] * 3 + [pltpu.SemaphoreType.DMA((2, WAVES, count))] * 4


def piece_rows(rows, count):
    return -(-rows // (WAVES * 2 * count * 16)) * 16


def back(second_part, shrink_part, early_part, *rest, heads, own):
    rows, width = second_part.shape
    count = lax.axis_size("dp") // 2
    inner = heads * HEAD_DIM
    early_shape = early_part.shape
    late_shape = (WAVES * 2 * count, piece_rows(4 * inner, count), width)
    padded = -(-inner // 128) * 128
    return pl.pallas_call(
        functools.partial(back_kernel, heads, own, count),
        in_specs=[VMEM] * 21,
        out_specs=[VMEM] * 5,
        out_shape=[
            jax.ShapeDtypeStruct((own, width), BF16),
            jax.ShapeDtypeStruct((own, width), F32),
            jax.ShapeDtypeStruct(early_shape, BF16),
            jax.ShapeDtypeStruct(late_shape, BF16),
            jax.ShapeDtypeStruct((8, width), F32),
        ],
        scratch_shapes=[
            pltpu.VMEM((rows, width), BF16),
            pltpu.VMEM((own, width), F32),
            pltpu.VMEM((1, width), F32),
            pltpu.VMEM((rows, width), BF16),
            pltpu.VMEM(late_shape, BF16),
            pltpu.VMEM((8, width), F32),
            pltpu.VMEM((rows, inner), BF16),
            pltpu.VMEM((inner, rows), BF16),
            pltpu.VMEM((padded, rows), F32),
            pltpu.VMEM((rows, inner), F32),
            pltpu.VMEM((rows, inner), F32),
            *exchange_scratch(1, own, width, True),
            *exchange_scratch(1, own, width, False),
            *exchange_scratch(1, own, width, False),
            *sum_scratch(*early_shape, count),
            *sum_scratch(*late_shape, count),
            pltpu.VMEM((4, 8, width), F32),
            pltpu.VMEM((2, 8, width), F32),
            pltpu.VMEM((count, 8, width), F32),
            pltpu.SemaphoreType.DMA((3 + count,)),
            pltpu.SemaphoreType.DMA((3 + count,)),
        ],
        compiler_params=pltpu.CompilerParams(
            collective_id=3, has_side_effects=True, vmem_limit_bytes=56 * 1024 * 1024
        ),
        name="back",
    )(second_part, shrink_part, early_part, *rest)


def to_payload(rows):
    count, width = lax.axis_size("dp") // 2, rows.shape[1]
    piece = piece_rows(rows.shape[0], count)
    units = WAVES * 2 * count
    padding = units * piece - rows.shape[0]
    return jnp.pad(rows, ((0, padding), (0, 0))).reshape(units, piece, width)


def half_turn(array):
    columns = array.reshape(array.shape[0], -1, 2, HEAD_DIM // 2)
    return np.stack([-columns[:, :, 1], columns[:, :, 0]], axis=2).reshape(array.shape)


def turn_matrix(width):
    return jnp.asarray(half_turn(np.eye(width, dtype=np.float32)), BF16)


def rotary_tables(rows, heads):
    half_width = HEAD_DIM // 2
    frequency = THETA ** (-(np.arange(half_width) * 2.0 / HEAD_DIM))
    angles = (np.arange(rows) % SEQ_LEN)[:, None] * frequency[None, :]
    angles = np.tile(angles, (1, 2 * heads))
    return jnp.asarray(np.cos(angles), F32), jnp.asarray(np.sin(angles), F32)


def on_device(
    tokens,
    first_gain,
    joint_weight,
    output_weight,
    second_gain,
    expand_weight,
    shrink_weight,
    cotangent,
):
    local_rows, model_width = tokens.shape
    own_rows = cotangent.shape[0]
    heads = joint_weight.shape[2] // HEAD_DIM
    inner = heads * HEAD_DIM
    units = expand_weight.shape[2]
    expand_flat = expand_weight.reshape(model_width, 2 * units)
    gain_one_row = first_gain.reshape(1, model_width)
    gain_two_row = second_gain.reshape(1, model_width)
    turn = turn_matrix(inner)

    grad_rows = lax.all_gather(cotangent, "tensor", axis=0, tiled=True)

    joint_parts = jnp.transpose(joint_weight, (1, 0, 2))
    turned = [dot(joint_parts[part], turn).astype(BF16)[None] for part in (0, 1)]
    cosine, sine = rotary_tables(local_rows, heads)
    second, middle, normed, key, key_t, query, query_t, value, mixed_t, logsum = front(
        tokens,
        gain_one_row,
        gain_two_row,
        jnp.concatenate([joint_parts, *turned], axis=0),
        output_weight,
        cosine,
        sine,
        heads=heads,
        own=own_rows,
    )
    gate_up = dot(second, expand_flat)

    def activate(gate_part, up_part):
        return jax.nn.gelu(gate_part, approximate=True) * up_part

    hidden, activate_back = jax.vjp(activate, gate_up[:, :units], gate_up[:, units:])
    hidden = hidden.astype(BF16)
    grad_hidden = dot(grad_rows, shrink_weight, ((1,), (1,)))
    grad_gate, grad_up = activate_back(grad_hidden)
    grad_both = jnp.concatenate([grad_gate, grad_up], axis=1).astype(BF16)
    second_part = dot(grad_both, expand_flat, ((1,), (1,))).astype(BF16)
    grad_shrink = dot(hidden, grad_rows, ((0,), (0,)))
    grad_expand = dot(grad_both, second, ((0,), (0,)))
    early = jnp.concatenate([grad_shrink, grad_expand], axis=0).astype(BF16)
    shrink_part = dot(hidden, shrink_weight).astype(BF16)
    block_out, grad_tokens, early, late, gains = back(
        second_part,
        shrink_part,
        to_payload(early),
        tokens,
        gain_one_row,
        gain_two_row,
        middle,
        cotangent,
        output_weight,
        joint_parts,
        normed,
        cosine,
        sine,
        turn,
        key,
        key_t,
        query,
        query_t,
        value,
        mixed_t,
        logsum,
        heads=heads,
        own=own_rows,
    )
    early = early.reshape(-1, model_width)
    late = late.reshape(-1, model_width)
    grad_value_w, grad_query_w, grad_key_w = (
        late[part * inner : (part + 1) * inner] for part in (1, 2, 3)
    )
    grad_joint_w = jnp.concatenate([grad_query_w, grad_key_w, grad_value_w], axis=0).astype(F32).T
    grad_expand = early[units : 3 * units].astype(F32).T
    return (
        block_out,
        grad_tokens,
        gains[0],
        grad_joint_w.reshape(model_width, 3, inner),
        late[:inner].astype(F32),
        gains[1],
        grad_expand.reshape(model_width, 2, units),
        early[:units].astype(F32),
    )


def solution(mesh):
    return jax.shard_map(
        on_device,
        mesh=mesh,
        in_specs=(
            P("dp", None),
            P(),
            P(None, None, "tensor"),
            P("tensor", None),
            P(),
            P(None, None, "tensor"),
            P("tensor", None),
            P(("dp", "tensor"), None),
        ),
        out_specs=(
            P(("dp", "tensor"), None),
            P(("dp", "tensor"), None),
            P(),
            P(None, None, "tensor"),
            P("tensor", None),
            P(),
            P(None, None, "tensor"),
            P("tensor", None),
        ),
        check_vma=False,
    )
```

```python
import functools

import jax
import jax.numpy as jnp
import numpy as np
from jax import lax
from jax.experimental import pallas as pl
from jax.experimental.pallas import tpu as pltpu
from jax.sharding import PartitionSpec as P

HEAD_DIM = 64
SEQ_LEN = 1024
EPS = 1e-05
THETA = 160000.0
SCALE = HEAD_DIM**-0.5
CHUNKS = 2
WAVES = 2
VMEM_LIMIT = 48 * 1024 * 1024
F32 = jnp.float32
BF16 = jnp.bfloat16
VMEM = pl.BlockSpec(memory_space=pltpu.VMEM)


def dot(a, b, dims=((1,), (0,))):
    return lax.dot_general(a, b, (dims, ((), ())), preferred_element_type=F32)


def norm_parts(values):
    centred = values - jnp.mean(values, axis=-1, keepdims=True)
    inverse = lax.rsqrt(jnp.mean(centred * centred, axis=-1, keepdims=True) + EPS)
    return centred * inverse, inverse


def norm_back(hat, inverse, gain, grad):
    scaled = grad * gain
    return inverse * (
        scaled
        - jnp.mean(scaled, axis=-1, keepdims=True)
        - hat * jnp.mean(scaled * hat, axis=-1, keepdims=True)
    )


def head_rows(array, head):
    index = lax.broadcasted_iota(jnp.int32, array.shape, 0) // HEAD_DIM
    return jnp.where(index == head, array, jnp.zeros_like(array))


def head_columns(array, head):
    index = lax.broadcasted_iota(jnp.int32, array.shape, 1) // HEAD_DIM
    return jnp.where(index == head, array, jnp.zeros_like(array))


def remote(src, dst, send_sem, recv_sem, target):
    copy = pltpu.make_async_remote_copy(
        src_ref=src,
        dst_ref=dst,
        send_sem=send_sem,
        recv_sem=recv_sem,
        device_id=target,
        device_id_type=pl.DeviceIdType.MESH,
    )
    copy.start()
    return copy


def greet(targets):
    barrier = pltpu.get_barrier_semaphore()
    for target in targets:
        pl.semaphore_signal(
            barrier, inc=1, device_id=target, device_id_type=pl.DeviceIdType.MESH
        )
    pl.semaphore_wait(barrier, len(targets))


class GroupSum:
    def __init__(self, parts, own, gather, scratch):
        self.parts, self.own, self.gather = parts, own, gather
        self.from_core, self.to_side, self.from_side = scratch[:3]
        self.core_send, self.core_recv, self.side_send, self.side_recv = scratch[3:]
        me = lax.axis_index("tensor")
        side, core = me // 2, me % 2
        self.me = me
        self.core_peer = side * 2 + (1 - core)
        self.side_peer = (1 - side) * 2 + core
        self.cross = (1 - side) * 2 + (1 - core)
        self.rows = own // CHUNKS
        self.unsent = []

    def peers(self):
        return [{"tensor": self.core_peer}, {"tensor": self.side_peer}]

    def at(self, owner, chunk):
        return pl.ds(pl.multiple_of(owner * self.own + chunk * self.rows, 16), self.rows)

    def here(self, chunk):
        return pl.ds(chunk * self.rows, self.rows)

    def to_core(self, src, dst, slot, chunk):
        sems = self.core_send.at[slot, chunk], self.core_recv.at[slot, chunk]
        copy = remote(src, dst, *sems, {"tensor": self.core_peer})
        self.unsent.append(copy)
        return copy

    def over(self, src, dst, slot, chunk):
        sems = self.side_send.at[slot, chunk], self.side_recv.at[slot, chunk]
        copy = remote(src, dst, *sems, {"tensor": self.side_peer})
        self.unsent.append(copy)
        return copy

    def start(self):
        self.start_onward()
        self.start_mine()

    def start_onward(self):
        self.onward = self.send_block(0, self.cross)

    def start_mine(self):
        self.mine = self.send_block(1, self.core_peer)

    def send_block(self, first, owner):
        return {
            (slot, chunk): self.to_core(
                part.at[self.at(owner, chunk)],
                self.from_core.at[2 * slot + first, self.here(chunk)],
                2 * slot + first,
                chunk,
            )
            for slot, part in enumerate(self.parts)
            for chunk in range(CHUNKS)
        }

    def cross_over(self):
        self.sideways = {}
        for slot, part in enumerate(self.parts):
            for chunk in range(CHUNKS):
                here = self.here(chunk)
                self.onward[slot, chunk].wait_recv()
                self.to_side[slot, here] = (
                    part[self.at(self.side_peer, chunk)].astype(F32)
                    + self.from_core[2 * slot, here].astype(F32)
                ).astype(BF16)
                self.sideways[slot, chunk] = self.over(
                    self.to_side.at[slot, here], self.from_side.at[slot, here], slot, chunk
                )

    def total(self, slot, chunk):
        here = self.here(chunk)
        self.mine[slot, chunk].wait_recv()
        self.sideways[slot, chunk].wait_recv()
        return (
            self.parts[slot][self.at(self.me, chunk)].astype(F32)
            + self.from_core[2 * slot + 1, here].astype(F32)
            + self.from_side[slot, here].astype(F32)
        )

    def totals(self, step, extra, outs):
        sums = len(self.parts)
        self.gathered = []
        for chunk in range(CHUNKS):
            totals = [self.total(slot, chunk) for slot in range(sums)]
            result = step(chunk, self.at(self.me, chunk), self.here(chunk), totals, extra, outs)
            if self.gather:
                outs[0][self.at(self.me, chunk), :] = result
                block = outs[0].at[self.at(self.me, chunk)]
                over = self.over(block, block, sums, chunk)
                near = self.to_core(block, block, 2 * sums, chunk)
                self.gathered.append((over, near))

    def spread(self, whole):
        sums = len(self.parts)
        relayed = []
        for chunk, (over, _) in enumerate(self.gathered):
            over.wait_recv()
            block = whole.at[self.at(self.side_peer, chunk)]
            relayed.append(self.to_core(block, block, 2 * sums + 1, chunk))
        for _, near in self.gathered:
            near.wait_recv()
        for relay in relayed:
            relay.wait_recv()

    def close(self):
        for copy in self.unsent:
            copy.wait_send()


def exchange_scratch(sums, own, width, gather):
    core_slots = 2 * sums + (2 if gather else 0)
    side_slots = sums + (1 if gather else 0)
    return [
        pltpu.VMEM((2 * sums, own, width), BF16),
        pltpu.VMEM((sums, own, width), BF16),
        pltpu.VMEM((sums, own, width), BF16),
        pltpu.SemaphoreType.DMA((core_slots, CHUNKS)),
        pltpu.SemaphoreType.DMA((core_slots, CHUNKS)),
        pltpu.SemaphoreType.DMA((side_slots, CHUNKS)),
        pltpu.SemaphoreType.DMA((side_slots, CHUNKS)),
    ]


def front_kernel(heads, own, *refs):
    tokens, gain_one, gain_two, joint, output_weight, cosine, sine = refs[:7]
    second, middle, normed, key, key_t, query, query_t, value, mixed_t, logsum = refs[7:17]
    value_t, branch_part = refs[17:19]
    group = GroupSum((branch_part,), own, True, refs[19:])
    greet(group.peers())
    rows = tokens.shape[0]

    def project(number, carry):
        down = pl.ds(pl.multiple_of(number * own, own), own)
        hat, _ = norm_parts(tokens[down, :].astype(F32))
        normal = (hat * gain_one[...]).astype(BF16)
        normed[down, :] = normal
        cos, sin = cosine[down, :], sine[down, :]
        turned = (dot(normal, joint[0]) * cos + dot(normal, joint[3]) * sin) * SCALE
        query[down, :] = turned.astype(BF16)
        query_t[:, down] = turned.T.astype(BF16)
        turned = dot(normal, joint[1]) * cos + dot(normal, joint[4]) * sin
        key[down, :] = turned.astype(BF16)
        key_t[:, down] = turned.T.astype(BF16)
        plain = dot(normal, joint[2])
        value[down, :] = plain.astype(BF16)
        value_t[:, down] = plain.T.astype(BF16)
        return carry

    lax.fori_loop(0, rows // own, project, 0)

    def attend(owner):
        down = pl.ds(pl.multiple_of(owner * own, own), own)
        for head in range(heads):
            part = slice(head * HEAD_DIM, (head + 1) * HEAD_DIM)
            scores = dot(key[...], head_rows(query_t[:, down], head))
            peak = jnp.max(scores, axis=0, keepdims=True)
            exps = jnp.exp(scores - peak)
            total = jnp.sum(exps, axis=0, keepdims=True)
            mixed = dot(value_t[part, :], exps.astype(BF16)) * (1.0 / total)
            mixed_t[part, down] = mixed.astype(BF16)
            logsum[head : head + 1, down] = peak + jnp.log(total)
        branch = dot(mixed_t[:, down], output_weight[...], ((0,), (0,)))
        branch_part[down, :] = branch.astype(BF16)

    attend(group.cross)
    group.start_onward()
    attend(group.side_peer)
    group.cross_over()
    attend(group.core_peer)
    group.start_mine()
    attend(group.me)
    group.totals(middle_step, (tokens, gain_two), (second, middle))
    group.spread(second)
    group.close()


def front(tokens, *rest, heads, own):
    rows, width = tokens.shape
    inner = heads * HEAD_DIM
    down, across = (rows, inner), (inner, rows)
    shapes = [
        ((rows, width), BF16),
        ((own, width), F32),
        ((rows, width), BF16),
        (down, BF16),
        (across, BF16),
        (down, BF16),
        (across, BF16),
        (down, BF16),
        (across, BF16),
        ((8, rows), F32),
    ]
    return pl.pallas_call(
        functools.partial(front_kernel, heads, own),
        in_specs=[VMEM] * 7,
        out_specs=[VMEM] * 10,
        out_shape=[jax.ShapeDtypeStruct(*shape) for shape in shapes],
        scratch_shapes=[
            pltpu.VMEM(across, BF16),
            pltpu.VMEM((rows, width), BF16),
            *exchange_scratch(1, own, width, True),
        ],
        compiler_params=pltpu.CompilerParams(
            collective_id=1, has_side_effects=True, vmem_limit_bytes=VMEM_LIMIT
        ),
        name="front",
    )(tokens, *rest)


def middle_step(chunk, rows, here, totals, extra, outs):
    tokens, gain = extra
    _, middle = outs
    value = tokens[rows, :].astype(F32) + totals[0]
    middle[here, :] = value
    hat, _ = norm_parts(value)
    return (hat * gain[...]).astype(BF16)


def middle_back_step(chunk, rows, here, totals, extra, outs):
    middle, gain, cotangent = extra
    _, grad_middle, grad_gain = outs
    hat, inverse = norm_parts(middle[here, :])
    value = cotangent[here, :].astype(F32) + norm_back(hat, inverse, gain[...], totals[0])
    grad_middle[here, :] = value
    term = jnp.sum(totals[0] * hat, axis=0, keepdims=True)
    if chunk == 0:
        grad_gain[...] = term
    else:
        grad_gain[...] += term
    return value.astype(BF16)


def token_step(chunk, rows, here, totals, extra, outs):
    tokens, gain, grad_middle = extra
    hat, inverse = norm_parts(tokens[rows, :].astype(F32))
    outs[0][here, :] = grad_middle[here, :] + norm_back(hat, inverse, gain[...], totals[0])


def out_step(chunk, rows, here, totals, extra, outs):
    outs[0][here, :] = (extra[0][here, :] + totals[0]).astype(BF16)


class DataSum:
    def __init__(self, payload, total, scratch):
        self.payload, self.result = payload, total
        self.from_pair, self.summed, self.arrived = scratch[:3]
        self.pair_send, self.pair_recv, self.far_send, self.far_recv = scratch[3:]
        self.waves, self.count = WAVES, payload.shape[0] // (2 * WAVES)
        data = lax.axis_index("dp")
        self.outer, self.inner = data // 2, data % 2
        self.near, self.spread, self.shared = {}, {}, {}
        self.unsent = []

    def pair(self):
        return {"dp": self.outer * 2 + (1 - self.inner)}

    def far(self, hop):
        return {"dp": (self.outer + hop) % self.count * 2 + self.inner}

    def peers(self):
        return [self.pair()] + [self.far(hop) for hop in range(1, self.count)]

    def unit(self, wave, inner, outer):
        return (wave * 2 + inner) * self.count + outer

    def place(self, hop):
        return (self.outer + hop) % self.count

    def behind(self, hop):
        return (self.outer + self.count - hop) % self.count

    def to_pair(self, src, dst, *sem):
        copy = remote(src, dst, self.pair_send.at[sem], self.pair_recv.at[sem], self.pair())
        self.unsent.append(copy)
        return copy

    def to_far(self, src, dst, hop, *sem):
        copy = remote(src, dst, self.far_send.at[sem], self.far_recv.at[sem], self.far(hop))
        self.unsent.append(copy)
        return copy

    def hops(self):
        return [*range(1, self.count), 0]

    def start(self, wave):
        for hop in self.hops():
            self.near[wave, hop] = self.to_pair(
                self.payload.at[self.unit(wave, 1 - self.inner, self.place(hop))],
                self.from_pair.at[wave, hop],
                0,
                wave,
                hop,
            )

    def scatter(self, wave):
        for hop in self.hops():
            self.near[wave, hop].wait_recv()
            self.summed[wave, hop] = (
                self.payload[self.unit(wave, self.inner, self.place(hop))].astype(F32)
                + self.from_pair[wave, hop].astype(F32)
            ).astype(BF16)
            if hop:
                self.spread[wave, hop] = self.to_far(
                    self.summed.at[wave, hop], self.arrived.at[wave, hop - 1], hop, 0, wave, hop
                )

    def collect(self, wave):
        value = self.summed[wave, 0].astype(F32)
        for hop in range(1, self.count):
            self.spread[wave, hop].wait_recv()
            value = value + self.arrived[wave, hop - 1].astype(F32)
        self.result[self.unit(wave, self.inner, self.outer)] = value.astype(BF16)
        block = self.result.at[self.unit(wave, self.inner, self.outer)]
        for hop in range(1, self.count):
            self.shared[wave, hop] = self.to_far(block, block, hop, 1, wave, hop)
        self.shared[wave, 0] = self.to_pair(block, block, 1, wave, 0)

    def relay(self, wave):
        for hop in range(1, self.count):
            self.shared[wave, hop].wait_recv()
            block = self.result.at[self.unit(wave, self.inner, self.behind(hop))]
            self.near[wave, hop] = self.to_pair(block, block, 1, wave, hop)

    def finish(self):
        for wave in range(self.waves):
            self.shared[wave, 0].wait_recv()
            for hop in range(1, self.count):
                self.near[wave, hop].wait_recv()

    def close(self):
        for copy in self.unsent:
            copy.wait_send()


class GainSum:
    def __init__(self, terms, total, group, data, scratch):
        self.terms, self.total, self.group, self.data = terms, total, group, data
        self.held, self.paired, self.outer = scratch[:3]
        self.send, self.recv = scratch[3:]
        self.unsent = []

    def copy(self, src, dst, target, sem):
        copy = remote(src, dst, self.send.at[sem], self.recv.at[sem], target)
        self.unsent.append(copy)
        return copy

    def start(self):
        me = self.group.me
        self.held[me] = self.terms[...]
        self.first = [
            self.copy(self.held.at[me], self.held.at[me], {"tensor": (me + hop) % 4}, hop - 1)
            for hop in range(1, 4)
        ]

    def pair_up(self):
        for copy in self.first:
            copy.wait_recv()
        self.paired[0] = (self.held[0] + self.held[1]) + (self.held[2] + self.held[3])
        self.second = self.copy(self.paired.at[0], self.paired.at[1], self.data.pair(), 3)

    def spread(self):
        self.second.wait_recv()
        outer = self.data.outer
        self.outer[outer] = self.paired[0] + self.paired[1]
        self.third = [
            self.copy(self.outer.at[outer], self.outer.at[outer], self.data.far(hop), 3 + hop)
            for hop in range(1, self.data.count)
        ]

    def finish(self):
        for copy in self.third:
            copy.wait_recv()
        value = self.outer[0]
        for number in range(1, self.data.count):
            value = value + self.outer[number]
        self.total[...] = value

    def close(self):
        for copy in self.unsent:
            copy.wait_send()


def back_kernel(heads, own, count, *refs):
    (
        second_part,
        shrink_part,
        early_part,
        tokens,
        gain_one,
        gain_two,
        middle,
        cotangent,
        output_weight,
        joint,
        normed,
        cosine,
        sine,
        turn,
        key,
        key_t,
        query,
        query_t,
        value,
        mixed_t,
        logsum,
    ) = refs[:21]
    block_out, grad_tokens, early_sum, late_sum, gains = refs[21:26]
    grad_branch, grad_middle, term_two, first_part, late_part, terms = refs[26:32]
    grad_mixed, grad_mixed_t, dq_t, dk, dv = refs[32:37]
    scratch = refs[37:]
    rows, width = tokens.shape
    inner = heads * HEAD_DIM
    block = 256

    norm_sum = GroupSum((second_part,), own, True, scratch[:7])
    out_sum = GroupSum((shrink_part,), own, False, scratch[7:14])
    token_sum = GroupSum((first_part,), own, False, scratch[14:21])
    early = DataSum(early_part, early_sum, scratch[21:28])
    late = DataSum(late_part, late_sum, scratch[28:35])
    gain = GainSum(terms, gains, norm_sum, early, scratch[35:40])
    greet(norm_sum.peers() + [{"tensor": norm_sum.cross}] + early.peers())

    norm_sum.start()
    early.start(0)
    early.start(1)
    norm_sum.cross_over()
    early.scatter(0)
    norm_sum.totals(
        middle_back_step,
        (middle, gain_two, cotangent),
        (grad_branch, grad_middle, term_two),
    )
    norm_sum.spread(grad_branch)
    early.scatter(1)
    out_sum.start()

    late_step = inner // late_part.shape[1]
    grad_output = dot(mixed_t[...], grad_branch[...]).astype(BF16)
    late_part[:late_step] = grad_output.reshape((late_step,) + late_part.shape[1:])
    grad_mixed[...] = dot(grad_branch[...], output_weight[...], ((1,), (1,))).astype(BF16)
    grad_mixed_t[...] = dot(output_weight[...], grad_branch[...], ((1,), (1,))).astype(BF16)
    dk[...] = jnp.zeros_like(dk)
    dv[...] = jnp.zeros_like(dv)
    early.collect(0)

    def attend_rows(number, carry):
        down = pl.ds(pl.multiple_of(number * block, block), block)
        for head in range(heads):
            part = slice(head * HEAD_DIM, (head + 1) * HEAD_DIM)
            scores = dot(key[...], head_rows(query_t[:, down], head))
            probs = jnp.exp(scores - logsum[head : head + 1, down])
            grad_t = grad_mixed_t[:, down]
            dprobs = dot(value[...], head_rows(grad_t, head))
            delta = jnp.sum(
                grad_mixed_t[part, down].astype(F32) * mixed_t[part, down].astype(F32),
                axis=0,
                keepdims=True,
            )
            dscores = (probs * (dprobs - delta)).astype(BF16)
            dq_t[part, down] = dot(key_t[part, :], dscores) * SCALE
            dk[...] += dot(dscores, head_columns(query[down, :], head))
            dv[...] += dot(probs.astype(BF16), head_columns(grad_mixed[down, :], head))
        return carry

    blocks = rows // block
    lax.fori_loop(0, blocks // 2, attend_rows, 0)
    out_sum.cross_over()
    early.collect(1)
    lax.fori_loop(blocks // 2, blocks, attend_rows, 0)
    early.relay(0)

    def turn_back(grad):
        moved = dot((grad * sine[...]).astype(BF16), turn[...], ((1,), (1,)))
        return (grad * cosine[...] + moved).astype(BF16)

    grad_parts = (turn_back(dq_t[...].T[:, :inner]), turn_back(dk[...]), dv[...].astype(BF16))
    units, piece, _ = late_part.shape
    step = inner // piece
    whole = units == 4 * step

    def keep(place, weight):
        kept = weight.astype(BF16).reshape(step, piece, width)
        late_part[place * step : (place + 1) * step] = kept

    if not whole:
        late_part[4 * step :] = jnp.zeros((units - 4 * step, piece, width), BF16)
    keep(1, dot(grad_parts[2], normed[...], ((0,), (0,))))
    if whole:
        late.start(0)
    keep(2, dot(grad_parts[0], normed[...], ((0,), (0,))))
    keep(3, dot(grad_parts[1], normed[...], ((0,), (0,))))
    if not whole:
        late.start(0)
    late.start(1)
    gain_term = jnp.zeros((1, width), F32)
    for owner in range(rows // own):
        here = slice(owner * own, (owner + 1) * own)
        value_rows = sum(
            dot(grad_parts[part][here], joint[part], ((1,), (1,))) for part in range(3)
        )
        first_part[here, :] = value_rows.astype(BF16)
        gain_term += jnp.sum(value_rows * normed[here, :].astype(F32), axis=0, keepdims=True)
    token_sum.start()
    early.relay(1)
    terms[...] = jnp.zeros_like(terms)
    terms[0:1, :] = gain_term / gain_one[...]
    terms[1:2, :] = term_two[...]
    gain.start()
    late.scatter(0)
    token_sum.cross_over()
    gain.pair_up()
    late.scatter(1)
    late.collect(0)
    out_sum.totals(out_step, (middle,), (block_out,))
    gain.spread()
    late.collect(1)
    token_sum.totals(token_step, (tokens, gain_one, grad_middle), (grad_tokens,))
    late.relay(0)
    late.relay(1)
    gain.finish()
    early.finish()
    late.finish()
    for work in (norm_sum, out_sum, token_sum, early, late, gain):
        work.close()


def sum_scratch(units, piece, width, count):
    held = pltpu.VMEM((WAVES, count, piece, width), BF16)
    return [held] * 3 + [pltpu.SemaphoreType.DMA((2, WAVES, count))] * 4


def piece_rows(rows, count):
    return -(-rows // (WAVES * 2 * count * 16)) * 16


def back(second_part, shrink_part, early_part, *rest, heads, own):
    rows, width = second_part.shape
    count = lax.axis_size("dp") // 2
    inner = heads * HEAD_DIM
    early_shape = early_part.shape
    late_shape = (WAVES * 2 * count, piece_rows(4 * inner, count), width)
    padded = -(-inner // 128) * 128
    return pl.pallas_call(
        functools.partial(back_kernel, heads, own, count),
        in_specs=[VMEM] * 21,
        out_specs=[VMEM] * 5,
        out_shape=[
            jax.ShapeDtypeStruct((own, width), BF16),
            jax.ShapeDtypeStruct((own, width), F32),
            jax.ShapeDtypeStruct(early_shape, BF16),
            jax.ShapeDtypeStruct(late_shape, BF16),
            jax.ShapeDtypeStruct((8, width), F32),
        ],
        scratch_shapes=[
            pltpu.VMEM((rows, width), BF16),
            pltpu.VMEM((own, width), F32),
            pltpu.VMEM((1, width), F32),
            pltpu.VMEM((rows, width), BF16),
            pltpu.VMEM(late_shape, BF16),
            pltpu.VMEM((8, width), F32),
            pltpu.VMEM((rows, inner), BF16),
            pltpu.VMEM((inner, rows), BF16),
            pltpu.VMEM((padded, rows), F32),
            pltpu.VMEM((rows, inner), F32),
            pltpu.VMEM((rows, inner), F32),
            *exchange_scratch(1, own, width, True),
            *exchange_scratch(1, own, width, False),
            *exchange_scratch(1, own, width, False),
            *sum_scratch(*early_shape, count),
            *sum_scratch(*late_shape, count),
            pltpu.VMEM((4, 8, width), F32),
            pltpu.VMEM((2, 8, width), F32),
            pltpu.VMEM((count, 8, width), F32),
            pltpu.SemaphoreType.DMA((3 + count,)),
            pltpu.SemaphoreType.DMA((3 + count,)),
        ],
        compiler_params=pltpu.CompilerParams(
            collective_id=3, has_side_effects=True, vmem_limit_bytes=56 * 1024 * 1024
        ),
        name="back",
    )(second_part, shrink_part, early_part, *rest)


def to_payload(rows):
    count, width = lax.axis_size("dp") // 2, rows.shape[1]
    piece = piece_rows(rows.shape[0], count)
    units = WAVES * 2 * count
    padding = units * piece - rows.shape[0]
    return jnp.pad(rows, ((0, padding), (0, 0))).reshape(units, piece, width)


def half_turn(array):
    columns = array.reshape(array.shape[0], -1, 2, HEAD_DIM // 2)
    return np.stack([-columns[:, :, 1], columns[:, :, 0]], axis=2).reshape(array.shape)


def turn_matrix(width):
    return jnp.asarray(half_turn(np.eye(width, dtype=np.float32)), BF16)


def rotary_tables(rows, heads):
    half_width = HEAD_DIM // 2
    frequency = THETA ** (-(np.arange(half_width) * 2.0 / HEAD_DIM))
    angles = (np.arange(rows) % SEQ_LEN)[:, None] * frequency[None, :]
    angles = np.tile(angles, (1, 2 * heads))
    return jnp.asarray(np.cos(angles), F32), jnp.asarray(np.sin(angles), F32)


def on_device(
    tokens,
    first_gain,
    joint_weight,
    output_weight,
    second_gain,
    expand_weight,
    shrink_weight,
    cotangent,
):
    local_rows, model_width = tokens.shape
    own_rows = cotangent.shape[0]
    heads = joint_weight.shape[2] // HEAD_DIM
    inner = heads * HEAD_DIM
    units = expand_weight.shape[2]
    expand_flat = expand_weight.reshape(model_width, 2 * units)
    gain_one_row = first_gain.reshape(1, model_width)
    gain_two_row = second_gain.reshape(1, model_width)
    turn = turn_matrix(inner)

    grad_rows = lax.all_gather(cotangent, "tensor", axis=0, tiled=True)

    joint_parts = jnp.transpose(joint_weight, (1, 0, 2))
    turned = [dot(joint_parts[part], turn).astype(BF16)[None] for part in (0, 1)]
    cosine, sine = rotary_tables(local_rows, heads)
    second, middle, normed, key, key_t, query, query_t, value, mixed_t, logsum = front(
        tokens,
        gain_one_row,
        gain_two_row,
        jnp.concatenate([joint_parts, *turned], axis=0),
        output_weight,
        cosine,
        sine,
        heads=heads,
        own=own_rows,
    )
    gate_up = dot(second, expand_flat)

    def activate(gate_part, up_part):
        return jax.nn.gelu(gate_part, approximate=True) * up_part

    hidden, activate_back = jax.vjp(activate, gate_up[:, :units], gate_up[:, units:])
    hidden = hidden.astype(BF16)
    grad_hidden = dot(grad_rows, shrink_weight, ((1,), (1,)))
    grad_gate, grad_up = activate_back(grad_hidden)
    grad_both = jnp.concatenate([grad_gate, grad_up], axis=1).astype(BF16)
    second_part = dot(grad_both, expand_flat, ((1,), (1,))).astype(BF16)
    grad_shrink = dot(hidden, grad_rows, ((0,), (0,)))
    grad_expand = dot(grad_both, second, ((0,), (0,)))
    early = jnp.concatenate([grad_shrink, grad_expand], axis=0).astype(BF16)
    shrink_part = dot(hidden, shrink_weight).astype(BF16)
    block_out, grad_tokens, early, late, gains = back(
        second_part,
        shrink_part,
        to_payload(early),
        tokens,
        gain_one_row,
        gain_two_row,
        middle,
        cotangent,
        output_weight,
        joint_parts,
        normed,
        cosine,
        sine,
        turn,
        key,
        key_t,
        query,
        query_t,
        value,
        mixed_t,
        logsum,
        heads=heads,
        own=own_rows,
    )
    early = early.reshape(-1, model_width)
    late = late.reshape(-1, model_width)
    grad_value_w, grad_query_w, grad_key_w = (
        late[part * inner : (part + 1) * inner] for part in (1, 2, 3)
    )
    grad_joint_w = jnp.concatenate([grad_query_w, grad_key_w, grad_value_w], axis=0).astype(F32).T
    grad_expand = early[units : 3 * units].astype(F32).T
    return (
        block_out,
        grad_tokens,
        gains[0],
        grad_joint_w.reshape(model_width, 3, inner),
        late[:inner].astype(F32),
        gains[1],
        grad_expand.reshape(model_width, 2, units),
        early[:units].astype(F32),
    )


def solution(mesh):
    return jax.shard_map(
        on_device,
        mesh=mesh,
        in_specs=(
            P("dp", None),
            P(),
            P(None, None, "tensor"),
            P("tensor", None),
            P(),
            P(None, None, "tensor"),
            P("tensor", None),
            P(("dp", "tensor"), None),
        ),
        out_specs=(
            P(("dp", "tensor"), None),
            P(("dp", "tensor"), None),
            P(),
            P(None, None, "tensor"),
            P("tensor", None),
            P(),
            P(None, None, "tensor"),
            P("tensor", None),
        ),
        check_vma=False,
    )
```
